128 devices in a mesh: blk: 8 (over x_hi, z), dp: 16 (over x_lo, y, core).
Axes of the slice: x: 4 (x_hi: 2, x_lo: 2; x = x_hi * 2 + x_lo), y: 4, z: 4, core: 2. Of those that a mesh axis runs over, the one named last changes fastest.
Arguments:
- queries: bfloat16 [16384, 3072], P(('blk', 'dp')), may hold values from -10.5 to 10.5
- positives: bfloat16 [16384, 3072], P(('blk', 'dp')), may hold values from -7 to 7
- corpus: bfloat16 [65536, 3072], P(('blk', 'dp')), may hold values from -6 to 6
- hard_ids: int32 [128, 12], P(('blk', 'dp')), may hold values from 0 to 511, as said below
Outputs:
- grad_queries: float32 [16384, 3072], P(('blk', 'dp'))
- grad_positives: float32 [16384, 3072], P(('blk', 'dp'))
- grad_corpus: float32 [65536, 3072], P(('blk', 'dp'))
- losses: float32 [16384], P(('blk', 'dp'))
The draws below stay inside these ranges and needn't reach their ends.
Inputs may be any that keep to these rules, and one draw needn't show every extreme that they name: `hard_ids`: the 12 ids of query block c name corpus blocks of 12 different device blocks that share the loop index of c: block h belongs to device block h // 4, whose loop index is h // 64.
All inputs are finite; a program needn't handle non-finite values.
Results may differ from the reference program's by a relative error of at most 0.0095.
Values may be sent and summed in bfloat16 or wider, within the bound.
No kernel may reach another device: no remote copies, remote signals or barrier semaphores. Data moves between devices by JAX's collectives and lax.ppermute only.
A program may use at most 192 MiB of HBM per device.

```python
import math
import jax
import jax.numpy as jnp
from jax import lax

D = 3072
Q_DEV = 128
BLOCK = 128
HB = 4
HN = 12
NQ = 16384
NH = 65536
N_BLK = 8
N_DP = 16


def shared_rows(key):
    return jnp.clip(jax.random.normal(key, (NQ, D), jnp.float32), -6.0, 6.0)


def draw_queries(key, part):
    key = jax.random.fold_in(key, 1)
    own_rows = jnp.clip(jax.random.normal(key, (NQ, D), jnp.float32), -6.0, 6.0)
    return own_rows.astype(jnp.bfloat16)


def draw_positives(key, part):
    base_rows = shared_rows(key)
    return base_rows.astype(jnp.bfloat16)


def draw_hard_ids(key, part):
    key = jax.random.fold_in(key, 3)
    first_key, second_key, third_key = jax.random.split(key, 3)
    block_count = NQ // BLOCK
    per_device = Q_DEV // BLOCK
    loop_of_row = jnp.arange(block_count, dtype=jnp.int32) // per_device // N_DP
    favour = jax.random.randint(first_key, (N_BLK, N_DP), 0, 8 * N_DP, dtype=jnp.int32)
    noise_scores = jax.random.randint(second_key, (block_count, N_DP), 0, 4 * N_DP, dtype=jnp.int32)
    ranking = (noise_scores + favour[loop_of_row]) * N_DP + jnp.arange(N_DP, dtype=jnp.int32)[None, :]
    owner_pick = lax.top_k(ranking, HN)[1].astype(jnp.int32)
    slot_pick = jax.random.randint(third_key, (block_count, HN), 0, HB, dtype=jnp.int32)
    return ((loop_of_row[:, None] * N_DP + owner_pick) * HB + slot_pick).astype(jnp.int32)


def block_scale(stream_key, dims, shards, low, high):
    def one(position, parts):
        draws = jax.random.uniform(jax.random.fold_in(jax.random.fold_in(stream_key, 6), position), (parts,), jnp.float32, low / len(shards), high / len(shards))
        return jnp.repeat(jnp.exp(draws), dims[position] // parts).reshape((-1,) + (1,) * (len(dims) - position - 1))

    loudness = one(*shards[0])
    for cut in shards[1:]:
        loudness = loudness * one(*cut)
    return loudness


def bell_draw(stream_key, dims, spread, bound, cuts=(), held_as=jnp.bfloat16):
    array = spread * jax.random.normal(stream_key, dims, jnp.float32)
    if cuts:
        array = array * block_scale(stream_key, dims, cuts, -0.22, 0.18)
    return jnp.clip(array, -bound, bound).astype(held_as)


def setup_inputs(seed: int = 0) -> dict:
    splits = jax.random.split(jax.random.key(seed), 5)
    queries = draw_queries(jax.random.fold_in(splits[4], 71), 0)
    positives = draw_positives(jax.random.fold_in(splits[4], 71), 0)
    corpus = bell_draw(splits[2], (NH, D), 1.0, 6.0, ((0, 128),))
    hard_ids = draw_hard_ids(jax.random.fold_in(splits[4], 71), 0)
    return dict(queries=queries, positives=positives, corpus=corpus, hard_ids=hard_ids)


scale_factor = 3.0
output_scale = 0.25

def padded_length(values):
    return lax.optimization_barrier(values.astype(jnp.bfloat16)).astype(jnp.float32)

def reference(queries, positives, corpus, hard_ids):
    query_blocks = Q_DEV // BLOCK
    device_count = N_BLK * N_DP
    multiplier = scale_factor / math.sqrt(D)
    corpus_table = corpus.reshape(HB * device_count, BLOCK, D)
    positive_grid = positives.reshape(N_BLK, N_DP, Q_DEV, D)
    query_grid = queries.reshape(device_count, Q_DEV, D)
    ids_grid = hard_ids.reshape(device_count, query_blocks, HN)
    row_index = jnp.arange(Q_DEV, dtype=jnp.int32)
    column_index = jnp.arange(N_BLK * Q_DEV, dtype=jnp.int32)

    def one_device(running, device):
        positive_acc, corpus_acc = running
        loop_index = (device // N_DP).astype(jnp.int32)
        group_index = (device % N_DP).astype(jnp.int32)
        local_queries = query_grid[device]
        loop_keys = lax.dynamic_index_in_dim(positive_grid, group_index, 1, keepdims=False).reshape(N_BLK * Q_DEV, D)
        local_ids = ids_grid[device]
        hard_negative_keys = corpus_table[local_ids]
        query_pieces = local_queries.reshape(query_blocks, BLOCK, D)
        inner_scores = jnp.dot(local_queries, loop_keys.T, preferred_element_type=jnp.float32) * multiplier
        hard_negative_scores = jnp.einsum('olw,omew->olme', query_pieces.astype(jnp.float32), hard_negative_keys.astype(jnp.float32)) * multiplier
        hard_flat = hard_negative_scores.reshape(Q_DEV, HN * BLOCK)
        row_peak = jnp.maximum(lax.optimization_barrier(jnp.max(inner_scores, axis=1)), lax.optimization_barrier(jnp.max(hard_flat, axis=1)))
        row_total = lax.optimization_barrier(jnp.sum(jnp.exp(inner_scores - row_peak[:, None]), axis=1)) + lax.optimization_barrier(jnp.sum(jnp.exp(hard_flat - row_peak[:, None]), axis=1))
        normaliser = row_peak + jnp.log(row_total)
        is_positive = column_index[None, :] == (loop_index * Q_DEV + row_index)[:, None]
        own_score = lax.optimization_barrier(jnp.sum(jnp.where(is_positive, inner_scores, 0.0), axis=1))
        losses = normaliser - own_score
        inner_weights = (jnp.exp(inner_scores - normaliser[:, None]) - is_positive.astype(jnp.float32)).astype(jnp.bfloat16)
        hard_negative_weights = jnp.exp(hard_negative_scores - normaliser.reshape(query_blocks, BLOCK)[:, :, None, None]).astype(jnp.bfloat16)
        block_parts = jnp.einsum('bqhk,bhkd->bqhd', hard_negative_weights.astype(jnp.float32), hard_negative_keys.astype(jnp.float32))
        query_grad = jnp.dot(inner_weights, loop_keys, preferred_element_type=jnp.float32)
        query_grad = query_grad + lax.optimization_barrier(jnp.sum(padded_length(block_parts), axis=2)).reshape(Q_DEV, D)
        positive_part = padded_length(jnp.dot(inner_weights.T, local_queries, preferred_element_type=jnp.float32))
        positive_acc = positive_acc.at[:, group_index].add(positive_part.reshape(N_BLK, Q_DEV, D))
        corpus_slice = padded_length(jnp.einsum('mfra,mfi->mrai', hard_negative_weights.astype(jnp.float32), query_pieces.astype(jnp.float32)))
        corpus_acc = corpus_acc.at[local_ids.reshape(-1)].add(corpus_slice.reshape(query_blocks * HN, BLOCK, D))
        return ((positive_acc, corpus_acc), (output_scale * query_grad, losses))
    start_state = (jnp.zeros((N_BLK, N_DP, Q_DEV, D), jnp.float32), jnp.zeros((HB * device_count, BLOCK, D), jnp.float32))
    final_state, stacked = lax.scan(one_device, start_state, jnp.arange(device_count, dtype=jnp.int32))
    grad_positives = output_scale * final_state[0].reshape(NQ, D)
    grad_corpus = output_scale * final_state[1].reshape(NH, D)
    grad_queries = stacked[0].reshape(NQ, D)
    losses = stacked[1].reshape(NQ)
    return (grad_queries, grad_positives, grad_corpus, losses)
```

```python
import math

import jax
import jax.numpy as jnp
from jax import lax
from jax.sharding import PartitionSpec as P

BLOCK = 128
SCALE = 3.0
OUT_SCALE = 0.25
LOW = -1e30
RING = 4


def dp_perm(move):
    pairs = []
    for i in range(16):
        a, b, c = move(i // 8, (i // 2) % 4, i % 2)
        pairs.append((i, (a % 2) * 8 + (b % 4) * 2 + c % 2))
    return pairs


def blk_perm(move):
    pairs = []
    for i in range(8):
        a, b = move(i // 4, i % 4)
        pairs.append((i, (a % 2) * 4 + b % 4))
    return pairs


class Plane:
    def __init__(self, axis):
        self.axis = axis
        if axis == "dp":
            self.up = dp_perm(lambda x, r, c: (x, r + 1, c))
            self.down = dp_perm(lambda x, r, c: (x, r - 1, c))
            self.across = dp_perm(lambda x, r, c: (x + 1, r, c))
        else:
            self.up = blk_perm(lambda x, r: (x, r + 1))
            self.down = blk_perm(lambda x, r: (x, r - 1))
            self.across = blk_perm(lambda x, r: (x + 1, r))

    def send(self, value, perm):
        return lax.ppermute(value, self.axis, perm)

    def gather(self, block):
        half = block.shape[0] // 2
        out = {}
        other = self.send(block, self.across)
        for dx, mine in ((0, block), (1, other)):
            out[dx, 0] = mine
            out[dx, 3] = self.send(mine, self.up)
            out[dx, 1] = self.send(mine, self.down)
            top = self.send(out[dx, 3][:half], self.up)
            bottom = self.send(out[dx, 1][half:], self.down)
            out[dx, 2] = jnp.concatenate([top, bottom], axis=0)
        return out

    def scatter(self, parts):
        done = {}
        for dx in (1, 0):
            half = parts[dx, 2].shape[0] // 2
            top = self.send(parts[dx, 2][:half], self.up)
            bottom = self.send(parts[dx, 2][half:], self.down)
            up = jnp.concatenate(
                [add(parts[dx, 1][:half], top), parts[dx, 1][half:].astype(jnp.float32)], axis=0
            ).astype(jnp.bfloat16)
            down = jnp.concatenate(
                [parts[dx, 3][:half].astype(jnp.float32), add(parts[dx, 3][half:], bottom)], axis=0
            ).astype(jnp.bfloat16)
            from_below = self.send(up, self.up)
            from_above = self.send(down, self.down)
            done[dx] = add(parts[dx, 0], from_below) + from_above.astype(jnp.float32)
            if dx == 1:
                across = self.send(done[1].astype(jnp.bfloat16), self.across)
        return done[0] + across.astype(jnp.float32)


def add(left, right):
    return left.astype(jnp.float32) + right.astype(jnp.float32)


def rows_dot(left, right):
    return lax.dot_general(left, right, (((1,), (1,)), ((), ())), preferred_element_type=jnp.float32)


def local(queries, positives, corpus, hard_ids):
    rows, width = queries.shape
    held = corpus.shape[0] // BLOCK
    group = lax.axis_size("dp")
    mult = SCALE / math.sqrt(width)
    dp, blk = Plane("dp"), Plane("blk")
    core_swap = dp_perm(lambda x, r, c: (x, r, c + 1))

    me = lax.axis_index("dp")
    offsets = [(dx, dr, dc) for dx in range(2) for dr in range(4) for dc in range(2)]
    mx, mr, mc = me // 8, (me // 2) % 4, me % 2
    rel_to_abs = jnp.stack(
        [((mx + a) % 2) * 8 + ((mr + b) % 4) * 2 + (mc + c) % 2 for a, b, c in offsets]
    )
    every = jnp.arange(16, dtype=jnp.int32)
    abs_to_rel = ((every // 8 - mx) % 2) * 8 + ((every // 2 % 4 - mr) % 4) * 2 + (every % 2 - mc) % 2

    keys = blk.gather(positives)
    qs = dp.gather(queries)
    gathered = {}
    for (dx, dr), value in qs.items():
        gathered[dx, dr, 0] = value
        gathered[dx, dr, 1] = dp.send(value, core_swap)

    owner = hard_ids // held % group
    slot = hard_ids % held
    matches = owner[0][:, None] == jnp.arange(group, dtype=jnp.int32)[None, :]
    wanted = jnp.sum(jnp.where(matches, slot[0][:, None] + 1, 0), axis=0) - 1
    asked = lax.all_to_all(wanted[:, None], "dp", split_axis=0, concat_axis=0, tiled=True)[:, 0]
    asked_rel = jnp.take(asked, rel_to_abs)

    table = corpus.reshape(held, BLOCK, width)
    picked = [
        lax.dynamic_index_in_dim(table, jnp.clip(asked_rel[j], 0, held - 1), 0, keepdims=False)
        for j in range(16)
    ]
    hard = jnp.stack([rows_dot(gathered[o], picked[j]) for j, o in enumerate(offsets)]) * mult
    hard = jnp.where((asked_rel >= 0)[:, None, None], hard, LOW)
    hard_peak = jnp.max(hard, axis=2)
    hard_total = jnp.where(
        (asked_rel >= 0)[:, None], jnp.sum(jnp.exp(hard - hard_peak[:, :, None]), axis=2), 0.0
    )

    loop_offsets = [(dx, dr) for dx in range(2) for dr in range(4)]
    inner = jnp.concatenate([rows_dot(queries, keys[o]) for o in loop_offsets], axis=1) * mult
    peak = jnp.max(inner, axis=1)
    total = jnp.sum(jnp.exp(inner - peak[:, None]), axis=1)
    row = lax.broadcasted_iota(jnp.int32, inner.shape, 0)
    col = lax.broadcasted_iota(jnp.int32, inner.shape, 1)
    diag = row == col
    own_score = jnp.sum(jnp.where(diag, inner, 0.0), axis=1)

    def merge(m1, s1, m2, s2):
        m = jnp.maximum(m1, m2)
        return m, s1 * jnp.exp(m1 - m) + s2 * jnp.exp(m2 - m)

    m0, s0 = merge(hard_peak[0], hard_total[0], peak, total)
    m = jnp.concatenate([m0[None], hard_peak[1:]], axis=0)
    s = jnp.concatenate([s0[None], hard_total[1:]], axis=0)
    state = jnp.take(jnp.stack([m, s], axis=1), abs_to_rel, axis=0)
    for move in (
        lambda x, r, c: (x, r, c + 1),
        lambda x, r, c: (x + 1, r, c),
        lambda x, r, c: (x, r ^ 1, c),
        lambda x, r, c: (x, r ^ 2, c),
    ):
        peer = lax.ppermute(state, "dp", dp_perm(move))
        m, s = merge(state[:, 0], state[:, 1], peer[:, 0], peer[:, 1])
        state = jnp.stack([m, s], axis=1)
    norm = jnp.take(state[:, 0] + jnp.log(state[:, 1]), rel_to_abs, axis=0)

    hard_w = jnp.exp(hard - norm[:, :, None]).astype(jnp.bfloat16)
    inner_w = (jnp.exp(inner - norm[0][:, None]) - diag.astype(jnp.float32)).astype(jnp.bfloat16)
    losses = norm[0] - own_score

    pos_parts = {}
    for j, o in enumerate(loop_offsets):
        pos_parts[o] = lax.dot_general(
            inner_w[:, j * BLOCK : (j + 1) * BLOCK],
            queries,
            (((0,), (0,)), ((), ())),
            preferred_element_type=jnp.float32,
        ).astype(jnp.bfloat16)
    grad_positives = OUT_SCALE * blk.scatter(pos_parts)

    part = {
        o: jnp.dot(hard_w[j], picked[j], preferred_element_type=jnp.float32).astype(jnp.bfloat16)
        for j, o in enumerate(offsets)
    }
    merged = {}
    for dx, dr in loop_offsets:
        merged[dx, dr] = add(part[dx, dr, 0], dp.send(part[dx, dr, 1], core_swap)).astype(jnp.bfloat16)
    hard_grad = dp.scatter(merged)
    loop_keys = jnp.concatenate([keys[o] for o in loop_offsets], axis=0)
    grad_queries = OUT_SCALE * (jnp.dot(inner_w, loop_keys, preferred_element_type=jnp.float32) + hard_grad)

    onehot = asked_rel[:, None] == jnp.arange(held, dtype=jnp.int32)[None, :]
    spread = jnp.where(onehot[:, None, :, None], hard_w[:, :, None, :], 0).reshape(16 * BLOCK, held * BLOCK)
    all_q = jnp.concatenate([gathered[o] for o in offsets], axis=0)
    grad_corpus = OUT_SCALE * lax.dot_general(
        spread, all_q, (((0,), (0,)), ((), ())), preferred_element_type=jnp.float32
    )
    return grad_queries, grad_positives, grad_corpus, losses


def solution(mesh):
    spec = P(("blk", "dp"), None)
    return jax.shard_map(
        local,
        mesh=mesh,
        in_specs=(spec,) * 4,
        out_specs=(spec, spec, spec, P(("blk", "dp"))),
        check_vma=False,
    )
```

```python
import math

import jax
import jax.numpy as jnp
from jax import lax
from jax.sharding import PartitionSpec as P

BLOCK = 128
HALF = 64
SCALE = 3.0
OUT_SCALE = 0.25
LOW = -1e30
AXES = ("blk", "dp")


def routes(move):
    pairs = []
    for i in range(128):
        b, d = i // 16, i % 16
        h, z, l, y, c = move(b // 4, b % 4, d // 8, (d // 2) % 4, d % 2)
        pairs.append((i, ((h % 2) * 4 + z % 4) * 16 + (l % 2) * 8 + (y % 4) * 2 + c % 2))
    return pairs


def way(c):
    return 1 - 2 * c


Y_FWD = routes(lambda h, z, l, y, c: (h, z, l, y + way(c), c))
Y_BWD = routes(lambda h, z, l, y, c: (h, z, l, y - way(c), c))
Z_FWD = routes(lambda h, z, l, y, c: (h, z + way(c), l, y, c))
Z_BWD = routes(lambda h, z, l, y, c: (h, z - way(c), l, y, c))
X_LO = routes(lambda h, z, l, y, c: (h, z, l + 1, y, c))
X_HI = routes(lambda h, z, l, y, c: (h + 1, z, l, y, c))
CORE = routes(lambda h, z, l, y, c: (h, z, l, y, c + 1))
Y_ONE = routes(lambda h, z, l, y, c: (h, z, l, y ^ 1, c))
Y_TWO = routes(lambda h, z, l, y, c: (h, z, l, y ^ 2, c))


def send(value, route):
    return lax.ppermute(value, AXES, route)


def after(value, *others):
    return lax.optimization_barrier((value, *others))[0]


def cat(*values):
    return jnp.concatenate(values, axis=0)


def add(left, right):
    return left.astype(jnp.float32) + right.astype(jnp.float32)


def rows_dot(left, right):
    return lax.dot_general(left, right, (((1,), (1,)), ((), ())), preferred_element_type=jnp.float32)


def cols_dot(left, right):
    return lax.dot_general(left, right, (((0,), (0,)), ((), ())), preferred_element_type=jnp.float32)


SPOTS = [(dx, dr) for dx in range(2) for dr in range(4)]


def scatter_first(parts, dx, fwd, bwd):
    top = send(parts[dx, 2][:HALF], fwd)
    bottom = send(parts[dx, 2][HALF:], bwd)
    return top, bottom


def scatter_second(parts, dx, top, bottom, fwd, bwd):
    ahead = cat(add(parts[dx, 1][:HALF], top), parts[dx, 1][HALF:].astype(jnp.float32))
    behind = cat(parts[dx, 3][:HALF].astype(jnp.float32), add(parts[dx, 3][HALF:], bottom))
    one = send(ahead.astype(jnp.bfloat16), fwd)
    two = send(behind.astype(jnp.bfloat16), bwd)
    return add(parts[dx, 0], one) + two.astype(jnp.float32)


def local(queries, positives, corpus, hard_ids):
    rows, width = queries.shape
    held = corpus.shape[0] // BLOCK
    mult = SCALE / math.sqrt(width)
    me = lax.axis_index("dp")
    mx, my, mc = me // 8, (me // 2) % 4, me % 2
    turn = 1 - 2 * mc

    x_q = send(queries, X_LO)
    q = {(0, 0): queries, (0, 3): send(queries, Y_FWD), (0, 1): send(queries, Y_BWD), (1, 0): x_q}
    p = {(0, 0): positives, (0, 3): send(positives, Z_FWD), (0, 1): send(positives, Z_BWD)}
    p[1, 0] = send(after(positives, x_q), X_HI)
    q[1, 3] = send(x_q, Y_FWD)
    q[1, 1] = send(x_q, Y_BWD)
    p[0, 2] = cat(send(p[0, 3][:HALF], Z_FWD), send(p[0, 1][HALF:], Z_BWD))
    other = send(after(corpus, q[0, 3]), CORE)
    y_top = send(cat(q[0, 3][:HALF], q[1, 3][:HALF]), Y_FWD)
    y_bottom = send(cat(q[0, 1][HALF:], q[1, 1][HALF:]), Y_BWD)
    q[0, 2] = cat(y_top[:HALF], y_bottom[:HALF])
    q[1, 2] = cat(y_top[HALF:], y_bottom[HALF:])
    p[1, 3] = send(p[1, 0], Z_FWD)
    p[1, 1] = send(p[1, 0], Z_BWD)
    p[1, 2] = cat(send(p[1, 3][:HALF], Z_FWD), send(p[1, 1][HALF:], Z_BWD))

    owner = hard_ids[0] // held % 16
    matches = owner[:, None] == jnp.arange(16, dtype=jnp.int32)[None, :]
    wanted = jnp.sum(jnp.where(matches, (hard_ids[0] % held)[:, None] + 1, 0), axis=0) - 1
    pairs = jnp.repeat(wanted.reshape(8, 1, 2), 2, axis=1).reshape(16, 2)
    asked = lax.all_to_all(pairs, "dp", split_axis=0, concat_axis=0, tiled=True)
    spot_place = jnp.stack([((mx + a) % 2) * 4 + (my + turn * b) % 4 for a, b in SPOTS])
    asked = jnp.take(asked.reshape(8, 2, 2), spot_place, axis=0)
    asked = lax.dynamic_index_in_dim(asked, mc, 1, keepdims=False)
    asked = jnp.where(mc == 0, asked, asked[:, ::-1])

    tables = (corpus.reshape(held, BLOCK, width), other.reshape(held, BLOCK, width))
    picked = {
        (j, w): lax.dynamic_index_in_dim(
            tables[w], jnp.clip(asked[j, w], 0, held - 1), 0, keepdims=False
        )
        for j in range(8)
        for w in range(2)
    }
    hard = jnp.stack(
        [jnp.stack([rows_dot(q[o], picked[j, w]) for w in range(2)]) for j, o in enumerate(SPOTS)]
    )
    asked_here = (asked >= 0)[:, :, None, None]
    hard = jnp.where(asked_here, hard * mult, LOW)
    hard_peak = jnp.max(hard, axis=(1, 3))
    hard_total = jnp.sum(
        jnp.where(asked_here, jnp.exp(hard - hard_peak[:, None, :, None]), 0.0), axis=(1, 3)
    )

    inner = jnp.concatenate([rows_dot(queries, p[o]) for o in SPOTS], axis=1) * mult
    peak = jnp.max(inner, axis=1)
    total = jnp.sum(jnp.exp(inner - peak[:, None]), axis=1)
    row = lax.broadcasted_iota(jnp.int32, inner.shape, 0)
    col = lax.broadcasted_iota(jnp.int32, inner.shape, 1)
    diag = row == col
    own_score = jnp.sum(jnp.where(diag, inner, 0.0), axis=1)

    def merge(m1, s1, m2, s2):
        m = jnp.maximum(m1, m2)
        return m, s1 * jnp.exp(m1 - m) + s2 * jnp.exp(m2 - m)

    m0, s0 = merge(hard_peak[0], hard_total[0], peak, total)
    every = jnp.arange(8, dtype=jnp.int32)
    place_spot = ((every // 4 - mx) % 2) * 4 + (turn * (every % 4 - my)) % 4
    state = jnp.stack([cat(m0[None], hard_peak[1:]), cat(s0[None], hard_total[1:])], axis=1)
    state = jnp.take(state, place_spot, axis=0)
    for route in (X_LO, Y_ONE, Y_TWO):
        peer = send(state, route)
        m, s = merge(state[:, 0], state[:, 1], peer[:, 0], peer[:, 1])
        state = jnp.stack([m, s], axis=1)
    norm = jnp.take(state[:, 0] + jnp.log(state[:, 1]), spot_place, axis=0)

    hard_w = jnp.exp(hard - norm[:, None, :, None]).astype(jnp.bfloat16)
    inner_w = (jnp.exp(inner - norm[0][:, None]) - diag.astype(jnp.float32)).astype(jnp.bfloat16)
    losses = norm[0] - own_score

    g_pos, g_hard = {}, {}
    for dx in (1, 0):
        for dr in (2, 1, 3, 0):
            j = SPOTS.index((dx, dr))
            g_hard[dx, dr] = (
                jnp.dot(hard_w[j, 0], picked[j, 0], preferred_element_type=jnp.float32)
                + jnp.dot(hard_w[j, 1], picked[j, 1], preferred_element_type=jnp.float32)
            ).astype(jnp.bfloat16)
            g_pos[dx, dr] = cols_dot(inner_w[:, j * BLOCK : (j + 1) * BLOCK], queries).astype(jnp.bfloat16)

    y1 = scatter_first(g_hard, 1, Y_FWD, Y_BWD)
    z1 = scatter_first(g_pos, 1, Z_FWD, Z_BWD)
    y_sum = scatter_second(g_hard, 1, *y1, Y_FWD, Y_BWD)
    z_sum = scatter_second(g_pos, 1, *z1, Z_FWD, Z_BWD)
    y0 = scatter_first(g_hard, 0, Y_FWD, Y_BWD)
    z0 = scatter_first(g_pos, 0, Z_FWD, Z_BWD)
    y_over = send(y_sum.astype(jnp.bfloat16), X_LO)
    z_over = send(z_sum.astype(jnp.bfloat16), X_HI)
    y_own = scatter_second(g_hard, 0, *y0, Y_FWD, Y_BWD)
    z_own = scatter_second(g_pos, 0, *z0, Z_FWD, Z_BWD)
    grad_positives = OUT_SCALE * add(z_own, z_over)
    loop_keys = cat(*[p[o] for o in SPOTS])
    grad_queries = OUT_SCALE * (
        jnp.dot(inner_w, loop_keys, preferred_element_type=jnp.float32) + add(y_own, y_over)
    )

    all_q = cat(*[q[o] for o in SPOTS])
    onehot = asked[:, :, None] == jnp.arange(held, dtype=jnp.int32)[None, None, :]
    spread = [
        jnp.where(onehot[:, w, None, :, None], hard_w[:, w, :, None, :], 0).reshape(8 * BLOCK, held * BLOCK)
        for w in range(2)
    ]
    theirs = send(cols_dot(spread[1], all_q).astype(jnp.bfloat16), CORE)
    grad_corpus = OUT_SCALE * (cols_dot(spread[0], all_q) + theirs.astype(jnp.float32))
    return grad_queries, grad_positives, grad_corpus, losses


def solution(mesh):
    spec = P(AXES, None)
    return jax.shard_map(
        local,
        mesh=mesh,
        in_specs=(spec,) * 4,
        out_specs=(spec, spec, spec, P(AXES)),
        check_vma=False,
    )
```

```python
import math

import jax
import jax.numpy as jnp
from jax import lax
from jax.experimental import pallas as pl
from jax.experimental.pallas import tpu as pltpu
from jax.sharding import PartitionSpec as P

BLOCK = 128
SCALE = 3.0
OUT_SCALE = 0.25
LOW = -1e30
CHUNK = 512
WIDE = 1024
AXES = ("blk", "dp")
F32 = jnp.float32
BF16 = jnp.bfloat16


def routes(move):
    pairs = []
    for i in range(128):
        b, d = i // 16, i % 16
        h, z, l, y, c = move(b // 4, b % 4, d // 8, (d // 2) % 4, d % 2)
        pairs.append((i, ((h % 2) * 4 + z % 4) * 16 + (l % 2) * 8 + (y % 4) * 2 + c % 2))
    return pairs


def way(c):
    return 1 - 2 * c


Y_FWD = routes(lambda h, z, l, y, c: (h, z, l, y + way(c), c))
Y_BWD = routes(lambda h, z, l, y, c: (h, z, l, y - way(c), c))
Z_FWD = routes(lambda h, z, l, y, c: (h, z + way(c), l, y, c))
Z_BWD = routes(lambda h, z, l, y, c: (h, z - way(c), l, y, c))
X_LO = routes(lambda h, z, l, y, c: (h, z, l + 1, y, c))
X_HI = routes(lambda h, z, l, y, c: (h + 1, z, l, y, c))
CORE = routes(lambda h, z, l, y, c: (h, z, l, y, c + 1))
Y_TWO = routes(lambda h, z, l, y, c: (h, z, l, y + 2, c))

SPOTS = [(dx, dr) for dx in range(2) for dr in range(4)]


def send(value, route):
    return lax.ppermute(value, AXES, route)


def after(value, *others):
    return lax.optimization_barrier((value, *others))[0]


def cat(*values):
    return jnp.concatenate(values, axis=0)


def rows_dot(left, right):
    return lax.dot_general(left, right, (((1,), (1,)), ((), ())), preferred_element_type=F32)


def mm(left, right):
    return jnp.dot(left, right, preferred_element_type=F32)


def near(value, *others):
    total = value.astype(F32)
    for other in others:
        total = total + other.astype(F32)
    return total


def column(array, chunk):
    if array.ndim == 2:
        return pl.BlockSpec((array.shape[0], chunk), lambda i, s: (0, i))
    return pl.BlockSpec((array.shape[0], array.shape[1], chunk), lambda i, s: (0, 0, i))


def kernel(body, slots, arrays, specs, out, out_spec, steps, scratch=()):
    return pl.pallas_call(
        body,
        grid_spec=pltpu.PrefetchScalarGridSpec(
            num_scalar_prefetch=1, grid=(steps,), in_specs=specs, out_specs=out_spec, scratch_shapes=scratch
        ),
        out_shape=out,
        compiler_params=pltpu.CompilerParams(vmem_limit_bytes=13 * 1024 * 1024),
        cost_estimate=pl.CostEstimate(flops=1024, bytes_accessed=1024, transcendentals=0),
    )(slots, *arrays)


def chosen(spot, w):
    return pl.BlockSpec((1, BLOCK, WIDE), lambda i, s: (jnp.maximum(s[2 * spot + w], 0), 0, i))


def whole(array):
    return pl.BlockSpec(array.shape, lambda i, s: (0,) * array.ndim)


def hard_scores(asked, tables, blocks, spots, mult):
    width = blocks[0].shape[1]
    count, steps = len(spots), width // WIDE

    def body(asked_ref, *refs):
        out, stats = refs[-2:]
        step = pl.program_id(0)

        @pl.when(step == 0)
        def _():
            out[...] = jnp.zeros_like(out)

        for n in range(count):
            query = refs[3 * n][...]
            for w in range(2):
                out[n, w] = out[n, w] + rows_dot(refs[3 * n + 1 + w][0], query)

        @pl.when(step == steps - 1)
        def _():
            for n, spot in enumerate(spots):
                scores = []
                for w in range(2):
                    score = jnp.where(asked_ref[2 * spot + w] >= 0, out[n, w] * mult, LOW)
                    out[n, w] = score
                    scores.append(score)
                peak = jnp.max(jnp.maximum(*scores), axis=0, keepdims=True)
                some = [jnp.where(score > 0.5 * LOW, jnp.exp(score - peak), 0.0) for score in scores]
                stats[n, 0:1] = peak
                stats[n, 1:2] = jnp.sum(some[0] + some[1], axis=0, keepdims=True)

    arrays, specs = [], []
    for block, spot in zip(blocks, spots):
        arrays += [block, *tables]
        specs += [column(block, WIDE), chosen(spot, 0), chosen(spot, 1)]
    outs = [jax.ShapeDtypeStruct((count, 2, BLOCK, BLOCK), F32), jax.ShapeDtypeStruct((count, 2, BLOCK), F32)]
    return kernel(body, asked, arrays, specs, outs, [whole(o) for o in outs], steps)


def hard_parts(asked, scores, norm, tables, plan, loop=()):
    width = tables[0].shape[2]
    count = len(plan)
    extra = [a for _, adds, _ in plan for a in adds]

    def body(asked_ref, norm_ref, *refs):
        mine, outs, held = refs[: 3 * count], refs[-count - 1 : -1], refs[-1]
        more = list(refs[3 * count : -count - 1])

        @pl.when(pl.program_id(0) == 0)
        def _():
            for n, (spot, _, _) in enumerate(plan):
                for w in range(2):
                    weight = jnp.exp(mine[3 * n][0, w] - norm_ref[spot : spot + 1, :])
                    held[n, :, w * BLOCK : (w + 1) * BLOCK] = weight.T.astype(BF16)

        for n, (_, adds, dtype) in enumerate(plan):
            keys = jnp.concatenate([mine[3 * n + 1][0], mine[3 * n + 2][0]], axis=0)
            total = mm(held[n], keys)
            for _ in adds:
                total = total + more.pop(0)[...].astype(F32)
            if n == 0 and loop:
                for m in range(len(loop) - 1):
                    total = total + mm(more[0][:, m * BLOCK : (m + 1) * BLOCK], more[m + 1][...])
            outs[n][...] = total.astype(dtype)

    arrays, specs = [], []
    for spot, _, _ in plan:
        array, n = scores[spot]
        arrays += [array, *tables]
        specs += [
            pl.BlockSpec((1, 2, BLOCK, BLOCK), lambda i, s, n=n: (n, 0, 0, 0)), chosen(spot, 0), chosen(spot, 1),
        ]
    arrays += extra + list(loop)
    specs += [column(a, WIDE) for a in extra] + [whole(a) for a in loop[:1]] + [column(a, WIDE) for a in loop[1:]]
    outs = [jax.ShapeDtypeStruct((BLOCK, width), dtype) for _, _, dtype in plan]
    return kernel(
        body, asked, (norm, *arrays), [whole(norm)] + specs, outs, [column(o, WIDE) for o in outs], width // WIDE,
        (pltpu.VMEM((count, BLOCK, 2 * BLOCK), BF16),),
    )


def corpus_part(asked, scores, norm, blocks, held, dtype, w, start=None):
    width = blocks[0].shape[1]
    count = len(blocks)
    arrays = []
    for array, _ in scores:
        if not any(array is a for a in arrays):
            arrays.append(array)
    place = [([array is a for a in arrays].index(True), n) for array, n in scores]

    def body(asked_ref, norm_ref, *refs):
        out, total, weights = refs[-3:]
        found, rest = refs[: len(arrays)], refs[len(arrays) :]

        @pl.when(pl.program_id(0) == 0)
        def _():
            for j, (k, n) in enumerate(place):
                weights[j] = jnp.exp(found[k][n, w] - norm_ref[j : j + 1, :]).astype(BF16)

        total[...] = jnp.zeros_like(total) if start is None else rest[count][...].astype(F32)
        for j in range(count):
            h = jnp.maximum(asked_ref[2 * j + w], 0)
            total[h] = total[h] + mm(weights[j], rest[j][...])
        out[...] = (total[...] * (1 if start is None else OUT_SCALE)).astype(dtype)

    more = () if start is None else (start,)
    out = jax.ShapeDtypeStruct((held, BLOCK, width), dtype)
    return kernel(
        body, asked, (norm, *arrays, *blocks, *more),
        [whole(a) for a in (norm, *arrays)] + [column(a, CHUNK) for a in (*blocks, *more)],
        out, column(out, CHUNK), width // CHUNK,
        (pltpu.VMEM((held, BLOCK, CHUNK), F32), pltpu.VMEM((count, BLOCK, BLOCK), BF16)),
    )


def local(queries, positives, corpus, hard_ids):
    rows, width = queries.shape
    held = corpus.shape[0] // BLOCK
    mult = SCALE / math.sqrt(width)
    me = lax.axis_index("dp")
    mx, my, mc = me // 8, (me // 2) % 4, me % 2
    turn = 1 - 2 * mc

    q, p = {(0, 0): queries}, {(0, 0): positives}
    other = send(corpus, CORE)
    q[1, 0] = send(queries, X_LO)
    q[0, 3], q[0, 1] = send(queries, Y_FWD), send(queries, Y_BWD)
    p[0, 3] = send(positives, Z_FWD)

    p[1, 0] = send(after(positives, q[1, 0], other), X_HI)
    q[1, 3] = send(after(q[1, 0], q[0, 3], other), Y_FWD)
    q[1, 1] = send(after(q[1, 0], q[0, 1], other), Y_BWD)
    p[0, 2] = send(after(p[0, 3], other), Z_FWD)
    p[0, 1] = send(after(positives, p[0, 3]), Z_BWD)

    q[0, 2] = send(after(q[0, 3], q[1, 3]), Y_FWD)
    q[1, 2] = send(q[1, 1], Y_BWD)
    p[1, 3], p[1, 1] = send(p[1, 0], Z_FWD), send(after(p[1, 0], p[0, 1]), Z_BWD)
    p[1, 2] = send(after(p[0, 2], p[1, 0]), X_HI)

    owner = hard_ids[0] // held % 16
    matches = owner[:, None] == jnp.arange(16, dtype=jnp.int32)[None, :]
    wanted = jnp.sum(jnp.where(matches, (hard_ids[0] % held)[:, None] + 1, 0), axis=0) - 1
    pairs = jnp.repeat(wanted.reshape(8, 1, 2), 2, axis=1).reshape(16, 2)
    asked = lax.all_to_all(after(pairs, q[1, 3]), "dp", split_axis=0, concat_axis=0, tiled=True)
    spot_place = jnp.stack([((mx + a) % 2) * 4 + (my + turn * b) % 4 for a, b in SPOTS])
    asked = jnp.take(asked.reshape(8, 2, 2), spot_place, axis=0)
    asked = lax.dynamic_index_in_dim(asked, mc, 1, keepdims=False)
    asked = jnp.where(mc == 0, asked, asked[:, ::-1])
    asked = after(jnp.clip(asked.reshape(16), -1, held - 1), p[1, 1])

    tables = (corpus.reshape(held, BLOCK, width), other.reshape(held, BLOCK, width))
    scores, stats = {}, {}
    for group in ([(0, 0), (1, 0), (0, 3), (0, 1), (1, 3), (1, 1)], [(0, 2), (1, 2)]):
        spots = [SPOTS.index(o) for o in group]
        out, stat = hard_scores(asked, tables, [q[o] for o in group], spots, mult)
        for n, j in enumerate(spots):
            scores[j], stats[j] = (out, n), stat[n]
    inner = cat(*[rows_dot(p[o], queries) for o in SPOTS]) * mult
    peak = jnp.max(inner, axis=0)
    total = jnp.sum(jnp.exp(inner - peak[None]), axis=0)
    row = lax.broadcasted_iota(jnp.int32, inner.shape, 0)
    col = lax.broadcasted_iota(jnp.int32, inner.shape, 1)
    diag = row == col
    own_score = jnp.sum(jnp.where(diag, inner, 0.0), axis=0)

    def merge(one, two):
        m = jnp.maximum(one[:, 0], two[:, 0])
        s = one[:, 1] * jnp.exp(one[:, 0] - m) + two[:, 1] * jnp.exp(two[:, 0] - m)
        return jnp.stack([m, s], axis=1)

    state = jnp.stack([stats[j] for j in range(8)])
    state = cat(merge(state[:1], jnp.stack([peak, total])[None]), state[1:])
    for route, turns in ((X_LO, (1, 0)), (Y_BWD, (0, 1)), (Y_TWO, (0, 2))):
        peer = send(state, route).reshape(2, 4, 2, BLOCK)
        state = merge(state, jnp.roll(peer, turns, axis=(0, 1)).reshape(8, 2, BLOCK))
    norm = state[:, 0] + jnp.log(state[:, 1])
    inner_w = (jnp.exp(inner - norm[:1]) - diag.astype(F32)).astype(BF16)
    losses = norm[0] - own_score

    def y_parts(wait, *plan, loop=()):
        return hard_parts(
            asked, scores, after(norm, *wait), tables, [(SPOTS.index(o), adds, dtype) for o, adds, dtype in plan], loop
        )

    def z_part(o, weights, *adds):
        j = SPOTS.index(o)
        return near(mm(weights[j * BLOCK : (j + 1) * BLOCK], queries), *adds).astype(BF16)

    y02, y12 = y_parts((), ((0, 2), (), BF16), ((1, 2), (), BF16))
    y02, y12 = send(y02, Y_FWD), send(y12, Y_BWD)
    z12 = send(z_part((1, 2), inner_w), X_HI)
    z11 = send(z_part((1, 1), inner_w), Z_FWD)
    z13 = send(z_part((1, 3), inner_w), Z_BWD)

    q_blocks = [q[o] for o in SPOTS]
    in_order = [scores[j] for j in range(8)]
    theirs = corpus_part(asked, in_order, norm, q_blocks, held, BF16, 1)
    inner_2 = after(inner_w, z12, z11, z13)
    y11, y13 = y_parts((y02, y12), ((1, 1), (), BF16), ((1, 3), (y12,), BF16))
    y11, y13 = send(y11, Y_FWD), send(y13, Y_BWD)
    z02 = send(z_part((0, 2), inner_2, z12), Z_FWD)
    z10 = send(z_part((1, 0), inner_2, z11, z13), X_HI)
    theirs = send(after(theirs, y02, y12, z12, z11, z13), CORE)

    inner_3 = after(inner_2, z02, z10)
    y10, y01, y03 = y_parts(
        (y11, y13, theirs), ((1, 0), (y11, y13), BF16), ((0, 1), (y02,), BF16), ((0, 3), (), BF16)
    )
    done = after(norm, y10)
    y10 = send(y10, X_LO)
    y01, y03 = send(y01, Y_FWD), send(y03, Y_BWD)
    z01 = send(z_part((0, 1), inner_3, z02), Z_FWD)
    z03 = send(z_part((0, 3), inner_3), Z_BWD)
    loop = (jnp.swapaxes(inner_3, 0, 1), *[p[o] for o in SPOTS])
    (mine,) = y_parts((done,), ((0, 0), (), F32), loop=loop)
    grad_corpus = corpus_part(asked, in_order, done, q_blocks, held, F32, 0, theirs)
    mine, first, grad_corpus = lax.optimization_barrier((mine, mm(inner_3[:BLOCK], queries), grad_corpus))
    grad_queries = OUT_SCALE * near(mine, y01, y03, y10)
    grad_positives = OUT_SCALE * near(first, z01, z03, z10)
    return grad_queries, grad_positives, grad_corpus.reshape(held * BLOCK, width), losses


def solution(mesh):
    spec = P(AXES, None)
    return jax.shard_map(
        local,
        mesh=mesh,
        in_specs=(spec,) * 4,
        out_specs=(spec, spec, spec, P(AXES)),
        check_vma=False,
    )
```

```python
import math

import jax
import jax.numpy as jnp
from jax import lax
from jax.experimental import pallas as pl
from jax.experimental.pallas import tpu as pltpu
from jax.sharding import PartitionSpec as P

BLOCK = 128
SCALE = 3.0
OUT_SCALE = 0.25
LOW = -1e30
CHUNK = 512
WIDE = 1024
AXES = ("blk", "dp")
F32 = jnp.float32
BF16 = jnp.bfloat16


def routes(move):
    pairs = []
    for i in range(128):
        b, d = i // 16, i % 16
        h, z, l, y, c = move(b // 4, b % 4, d // 8, (d // 2) % 4, d % 2)
        pairs.append((i, ((h % 2) * 4 + z % 4) * 16 + (l % 2) * 8 + (y % 4) * 2 + c % 2))
    return pairs


def way(c):
    return 1 - 2 * c


Y_FWD = routes(lambda h, z, l, y, c: (h, z, l, y + way(c), c))
Y_BWD = routes(lambda h, z, l, y, c: (h, z, l, y - way(c), c))
Z_FWD = routes(lambda h, z, l, y, c: (h, z + way(c), l, y, c))
Z_BWD = routes(lambda h, z, l, y, c: (h, z - way(c), l, y, c))
X_LO = routes(lambda h, z, l, y, c: (h, z, l + 1, y, c))
X_HI = routes(lambda h, z, l, y, c: (h + 1, z, l, y, c))
CORE = routes(lambda h, z, l, y, c: (h, z, l, y, c + 1))
Y_TWO = routes(lambda h, z, l, y, c: (h, z, l, y + 2, c))

SPOTS = [(dx, dr) for dx in range(2) for dr in range(4)]


def send(value, route):
    return lax.ppermute(value, AXES, route)


def after(value, *others):
    return lax.optimization_barrier((value, *others))[0]


def cat(*values):
    return jnp.concatenate(values, axis=0)


def rows_dot(left, right):
    return lax.dot_general(left, right, (((1,), (1,)), ((), ())), preferred_element_type=F32)


def mm(left, right):
    return jnp.dot(left, right, preferred_element_type=F32)


def near(value, *others):
    total = value.astype(F32)
    for other in others:
        total = total + other.astype(F32)
    return total


def column(array, chunk):
    if array.ndim == 2:
        return pl.BlockSpec((array.shape[0], chunk), lambda i, s: (0, i))
    return pl.BlockSpec((array.shape[0], array.shape[1], chunk), lambda i, s: (0, 0, i))


def kernel(body, slots, arrays, specs, out, out_spec, steps, scratch=()):
    return pl.pallas_call(
        body,
        grid_spec=pltpu.PrefetchScalarGridSpec(
            num_scalar_prefetch=1, grid=(steps,), in_specs=specs, out_specs=out_spec, scratch_shapes=scratch
        ),
        out_shape=out,
        compiler_params=pltpu.CompilerParams(vmem_limit_bytes=13 * 1024 * 1024),
        cost_estimate=pl.CostEstimate(flops=1024, bytes_accessed=1024, transcendentals=0),
    )(slots, *arrays)


def chosen(spot, w):
    return pl.BlockSpec((1, BLOCK, WIDE), lambda i, s: (jnp.maximum(s[2 * spot + w], 0), 0, i))


def whole(array):
    return pl.BlockSpec(array.shape, lambda i, s: (0,) * array.ndim)


def hard_scores(asked, tables, blocks, spots, mult):
    width = blocks[0].shape[1]
    count, steps = len(spots), width // WIDE

    def body(asked_ref, *refs):
        out, stats = refs[-2:]
        step = pl.program_id(0)

        @pl.when(step == 0)
        def _():
            out[...] = jnp.zeros_like(out)

        for n in range(count):
            query = refs[3 * n][...]
            for w in range(2):
                out[n, w] = out[n, w] + rows_dot(refs[3 * n + 1 + w][0], query)

        @pl.when(step == steps - 1)
        def _():
            for n, spot in enumerate(spots):
                scores = []
                for w in range(2):
                    score = jnp.where(asked_ref[2 * spot + w] >= 0, out[n, w] * mult, LOW)
                    out[n, w] = score
                    scores.append(score)
                peak = jnp.max(jnp.maximum(*scores), axis=0, keepdims=True)
                some = [jnp.where(score > 0.5 * LOW, jnp.exp(score - peak), 0.0) for score in scores]
                stats[n, 0:1] = peak
                stats[n, 1:2] = jnp.sum(some[0] + some[1], axis=0, keepdims=True)

    arrays, specs = [], []
    for block, spot in zip(blocks, spots):
        arrays += [block, *tables]
        specs += [column(block, WIDE), chosen(spot, 0), chosen(spot, 1)]
    outs = [jax.ShapeDtypeStruct((count, 2, BLOCK, BLOCK), F32), jax.ShapeDtypeStruct((count, 2, BLOCK), F32)]
    return kernel(body, asked, arrays, specs, outs, [whole(o) for o in outs], steps)


def hard_parts(asked, scores, norm, tables, plan, peers=None, loop=()):
    width = tables[0].shape[2]
    count = len(plan)
    extra = [a for _, adds, _ in plan for a, _ in adds]
    tail = (() if peers is None else (peers,)) + tuple(loop)

    def body(asked_ref, norm_ref, *refs):
        mine, outs, held = refs[: 3 * count], refs[-count - 1 : -1], refs[-1]
        more = list(refs[3 * count : 3 * count + len(extra)])
        rest = list(refs[3 * count + len(extra) : -count - 1])
        peers_ref = None if peers is None else rest.pop(0)

        @pl.when(pl.program_id(0) == 0)
        def _():
            for n, (spot, _, _) in enumerate(plan):
                for w in range(2):
                    score = mine[3 * n][0, w]
                    weight = jnp.where(score > 0.5 * LOW, jnp.exp(score - norm_ref[spot : spot + 1, :]), 0.0)
                    held[n, :, w * BLOCK : (w + 1) * BLOCK] = weight.T.astype(BF16)

        for n, (spot, adds, dtype) in enumerate(plan):
            keys = jnp.concatenate([mine[3 * n + 1][0], mine[3 * n + 2][0]], axis=0)
            total = mm(held[n], keys)
            for _, peer in adds:
                piece = more.pop(0)[...].astype(F32)
                if peer is not None:
                    scale = jnp.exp(peers_ref[peer : peer + 1, :] - norm_ref[spot : spot + 1, :])
                    piece = piece * jnp.broadcast_to(scale, (BLOCK, BLOCK)).T[:, :1]
                total = total + piece
            if n == 0 and loop:
                for m in range(len(loop) - 1):
                    total = total + mm(rest[0][:, m * BLOCK : (m + 1) * BLOCK], rest[m + 1][...])
            outs[n][...] = total.astype(dtype)

    arrays, specs = [], []
    for spot, _, _ in plan:
        array, n = scores[spot]
        arrays += [array, *tables]
        specs += [
            pl.BlockSpec((1, 2, BLOCK, BLOCK), lambda i, s, n=n: (n, 0, 0, 0)), chosen(spot, 0), chosen(spot, 1),
        ]
    arrays += extra + list(tail)
    specs += [column(a, WIDE) for a in extra] + [whole(a) for a in tail[: len(tail) - max(len(loop) - 1, 0)]]
    specs += [column(a, WIDE) for a in loop[1:]]
    outs = [jax.ShapeDtypeStruct((BLOCK, width), dtype) for _, _, dtype in plan]
    return kernel(
        body, asked, (norm, *arrays), [whole(norm)] + specs, outs, [column(o, WIDE) for o in outs], width // WIDE,
        (pltpu.VMEM((count, BLOCK, 2 * BLOCK), BF16),),
    )


def corpus_part(asked, scores, norm, blocks, held, dtype, w, start=None):
    width = blocks[0].shape[1]
    count = len(blocks)
    arrays = []
    for array, _ in scores:
        if not any(array is a for a in arrays):
            arrays.append(array)
    place = [([array is a for a in arrays].index(True), n) for array, n in scores]

    def body(asked_ref, norm_ref, *refs):
        out, total, weights = refs[-3:]
        found, rest = refs[: len(arrays)], refs[len(arrays) :]

        @pl.when(pl.program_id(0) == 0)
        def _():
            for j, (k, n) in enumerate(place):
                score = found[k][n, w]
                weight = jnp.where(score > 0.5 * LOW, jnp.exp(score - norm_ref[j : j + 1, :]), 0.0)
                weights[j] = weight.astype(BF16)

        total[...] = jnp.zeros_like(total) if start is None else rest[count][...].astype(F32)
        for j in range(count):
            h = jnp.maximum(asked_ref[2 * j + w], 0)
            total[h] = total[h] + mm(weights[j], rest[j][...])
        out[...] = (total[...] * (1 if start is None else OUT_SCALE)).astype(dtype)

    more = () if start is None else (start,)
    out = jax.ShapeDtypeStruct((held, BLOCK, width), dtype)
    return kernel(
        body, asked, (norm, *arrays, *blocks, *more),
        [whole(a) for a in (norm, *arrays)] + [column(a, CHUNK) for a in (*blocks, *more)],
        out, column(out, CHUNK), width // CHUNK,
        (pltpu.VMEM((held, BLOCK, CHUNK), F32), pltpu.VMEM((count, BLOCK, BLOCK), BF16)),
    )


def local(queries, positives, corpus, hard_ids):
    rows, width = queries.shape
    held = corpus.shape[0] // BLOCK
    mult = SCALE / math.sqrt(width)
    me = lax.axis_index("dp")
    mx, my, mc = me // 8, (me // 2) % 4, me % 2
    turn = 1 - 2 * mc

    owner = hard_ids[0] // held % 16
    matches = owner[:, None] == jnp.arange(16, dtype=jnp.int32)[None, :]
    wanted = jnp.sum(jnp.where(matches, (hard_ids[0] % held)[:, None] + 1, 0), axis=0) - 1
    pairs = jnp.repeat(wanted.reshape(8, 1, 2), 2, axis=1).reshape(16, 2)
    asked = lax.all_to_all(pairs, "dp", split_axis=0, concat_axis=0, tiled=True)
    spot_place = jnp.stack([((mx + a) % 2) * 4 + (my + turn * b) % 4 for a, b in SPOTS])
    asked = jnp.take(asked.reshape(8, 2, 2), spot_place, axis=0)
    asked = lax.dynamic_index_in_dim(asked, mc, 1, keepdims=False)
    asked = jnp.where(mc == 0, asked, asked[:, ::-1])
    asked = jnp.clip(asked.reshape(16), -1, held - 1)

    q, p = {(0, 0): queries}, {(0, 0): positives}
    other = send(corpus, CORE)
    q[1, 0] = send(queries, X_LO)
    q[0, 3], q[0, 1] = send(queries, Y_FWD), send(queries, Y_BWD)
    p[0, 3] = send(after(positives, asked), Z_FWD)

    p[1, 0] = send(after(positives, q[1, 0], other), X_HI)
    q[1, 3] = send(after(q[1, 0], other), Y_FWD)
    q[1, 1] = send(after(q[1, 0], other), Y_BWD)
    p[0, 2] = send(after(p[0, 3], other), Z_FWD)
    p[0, 1] = send(after(positives, q[0, 1], q[0, 3], other), Z_BWD)

    q[0, 2] = send(after(q[0, 3], q[1, 3]), Y_FWD)
    q[1, 2] = send(q[1, 1], Y_BWD)
    p[1, 3], p[1, 1] = send(p[1, 0], Z_FWD), send(after(p[1, 0], p[0, 1]), Z_BWD)
    p[1, 2] = send(after(p[0, 2], p[1, 0]), X_HI)


    tables = (corpus.reshape(held, BLOCK, width), other.reshape(held, BLOCK, width))
    scores, stats = {}, {}
    for group in ([(0, 0), (1, 0), (0, 3), (0, 1), (1, 3), (1, 1)], [(0, 2), (1, 2)]):
        spots = [SPOTS.index(o) for o in group]
        out, stat = hard_scores(asked, tables, [q[o] for o in group], spots, mult)
        for n, j in enumerate(spots):
            scores[j], stats[j] = (out, n), stat[n]
    inner = cat(*[rows_dot(p[o], queries) for o in SPOTS]) * mult
    peak = jnp.max(inner, axis=0)
    total = jnp.sum(jnp.exp(inner - peak[None]), axis=0)
    row = lax.broadcasted_iota(jnp.int32, inner.shape, 0)
    col = lax.broadcasted_iota(jnp.int32, inner.shape, 1)
    diag = row == col
    own_score = jnp.sum(jnp.where(diag, inner, 0.0), axis=0)

    def merge(one, two):
        m = jnp.maximum(one[:, 0], two[:, 0])
        s = one[:, 1] * jnp.exp(one[:, 0] - m) + two[:, 1] * jnp.exp(two[:, 0] - m)
        return jnp.stack([m, s], axis=1)

    state = jnp.stack([stats[j] for j in range(8)])
    peaks = state[:, 0]
    near_spot, far_spot = SPOTS.index((0, 2)), SPOTS.index((1, 2))
    state = cat(merge(state[:1], jnp.stack([peak, total])[None]), state[1:])

    def turned(peer, turns):
        return jnp.roll(peer.reshape(2, 4, 2, BLOCK), turns, axis=(0, 1)).reshape(8, 2, BLOCK)

    state = merge(state, turned(send(state, X_LO), (1, 0)))
    behind = send(cat(state, stats[near_spot][None]), Y_FWD)
    ahead = send(cat(state, stats[far_spot][None]), Y_BWD)
    across = send(state, Y_TWO)
    peers = cat(behind[8:, 0], ahead[8:, 0])
    state = merge(merge(state, turned(ahead[:8], (0, 1))), merge(turned(behind[:8], (0, 3)), turned(across, (0, 2))))
    norm = state[:, 0] + jnp.log(state[:, 1])
    inner_w = (jnp.exp(inner - norm[:1]) - diag.astype(F32)).astype(BF16)
    losses = norm[0] - own_score

    def y_parts(reference, wait, *plan, **more):
        return hard_parts(
            asked, scores, after(reference, *wait), tables,
            [(SPOTS.index(o), adds, dtype) for o, adds, dtype in plan], **more
        )

    def z_part(o, weights, *adds):
        j = SPOTS.index(o)
        return near(mm(weights[j * BLOCK : (j + 1) * BLOCK], queries), *adds).astype(BF16)

    y02, y12 = y_parts(peaks, (), ((0, 2), (), BF16), ((1, 2), (), BF16))
    y02, y12 = send(after(y02, across), Y_FWD), send(after(y12, across), Y_BWD)
    z12 = send(z_part((1, 2), inner_w), X_HI)
    z11 = send(z_part((1, 1), inner_w), Z_FWD)
    z13 = send(z_part((1, 3), inner_w), Z_BWD)

    q_blocks = [q[o] for o in SPOTS]
    in_order = [scores[j] for j in range(8)]
    theirs = corpus_part(asked, in_order, norm, q_blocks, held, BF16, 1)
    y11, y13 = y_parts(norm, (y02, y12), ((1, 1), (), BF16), ((1, 3), ((y12, 1),), BF16), peers=peers)
    inner_2 = after(inner_w, y11)
    y11, y13 = send(y11, Y_FWD), send(y13, Y_BWD)
    z02 = send(z_part((0, 2), inner_2, z12), Z_FWD)
    z10 = send(z_part((1, 0), inner_2, z11, z13), X_HI)
    theirs = send(after(theirs, inner_2, z12, z11, z13), CORE)

    inner_3 = after(inner_2, z02, theirs)
    z01 = send(z_part((0, 1), inner_3, z02), Z_FWD)
    z03 = send(z_part((0, 3), inner_3), Z_BWD)
    loop = (jnp.swapaxes(inner_3, 0, 1), *[p[o] for o in SPOTS])
    (mine,) = y_parts(norm, (z02, theirs), ((0, 0), (), F32), loop=loop)
    y10, y01, y03 = y_parts(
        norm, (y11, y13, mine), ((1, 0), ((y11, None), (y13, None)), BF16), ((0, 1), ((y02, 0),), BF16),
        ((0, 3), (), BF16), peers=peers
    )
    y10 = send(after(y10, z10), X_LO)
    y01, y03 = send(y01, Y_FWD), send(y03, Y_BWD)
    grad_corpus = corpus_part(asked, in_order, after(norm, z03), q_blocks, held, F32, 0, theirs)
    mine, first, grad_corpus = lax.optimization_barrier((mine, mm(inner_3[:BLOCK], queries), grad_corpus))
    grad_queries = OUT_SCALE * near(mine, y01, y03, y10)
    grad_positives = OUT_SCALE * near(first, z01, z03, z10)
    return grad_queries, grad_positives, grad_corpus.reshape(held * BLOCK, width), losses


def solution(mesh):
    spec = P(AXES, None)
    return jax.shard_map(
        local,
        mesh=mesh,
        in_specs=(spec,) * 4,
        out_specs=(spec, spec, spec, P(AXES)),
        check_vma=False,
    )
```

```python
import math

import jax
import jax.numpy as jnp
from jax import lax
from jax.experimental import pallas as pl
from jax.experimental.pallas import tpu as pltpu
from jax.sharding import PartitionSpec as P

BLOCK = 128
SCALE = 3.0
OUT_SCALE = 0.25
LOW = -1e30
CHUNK = 512
WIDE = 1536
AXES = ("blk", "dp")
F32 = jnp.float32
BF16 = jnp.bfloat16


def routes(move):
    pairs = []
    for i in range(128):
        b, d = i // 16, i % 16
        h, z, l, y, c = move(b // 4, b % 4, d // 8, (d // 2) % 4, d % 2)
        pairs.append((i, ((h % 2) * 4 + z % 4) * 16 + (l % 2) * 8 + (y % 4) * 2 + c % 2))
    return pairs


def way(c):
    return 1 - 2 * c


Y_FWD = routes(lambda h, z, l, y, c: (h, z, l, y + way(c), c))
Y_BWD = routes(lambda h, z, l, y, c: (h, z, l, y - way(c), c))
Z_FWD = routes(lambda h, z, l, y, c: (h, z + way(c), l, y, c))
Z_BWD = routes(lambda h, z, l, y, c: (h, z - way(c), l, y, c))
X_LO = routes(lambda h, z, l, y, c: (h, z, l + 1, y, c))
X_HI = routes(lambda h, z, l, y, c: (h + 1, z, l, y, c))
CORE = routes(lambda h, z, l, y, c: (h, z, l, y, c + 1))
Y_TWO = routes(lambda h, z, l, y, c: (h, z, l, y + 2, c))

SPOTS = [(dx, dr) for dx in range(2) for dr in range(4)]


def send(value, route):
    return lax.ppermute(value, AXES, route)


def after(value, *others):
    return lax.optimization_barrier((value, *others))[0]


def cat(*values):
    return jnp.concatenate(values, axis=0)


def rows_dot(left, right):
    return lax.dot_general(left, right, (((1,), (1,)), ((), ())), preferred_element_type=F32)


def mm(left, right):
    return jnp.dot(left, right, preferred_element_type=F32)


def near(value, *others):
    total = value.astype(F32)
    for other in others:
        total = total + other.astype(F32)
    return total


def column(array, chunk):
    if array.ndim == 2:
        return pl.BlockSpec((array.shape[0], chunk), lambda i, s: (0, i))
    return pl.BlockSpec((array.shape[0], array.shape[1], chunk), lambda i, s: (0, 0, i))


def kernel(body, slots, arrays, specs, out, out_spec, steps, scratch=()):
    return pl.pallas_call(
        body,
        grid_spec=pltpu.PrefetchScalarGridSpec(
            num_scalar_prefetch=1, grid=(steps,), in_specs=specs, out_specs=out_spec, scratch_shapes=scratch
        ),
        out_shape=out,
        compiler_params=pltpu.CompilerParams(vmem_limit_bytes=18 * 1024 * 1024),
        cost_estimate=pl.CostEstimate(flops=1024, bytes_accessed=1024, transcendentals=0),
    )(slots, *arrays)


def chosen(spot, w):
    return pl.BlockSpec((1, BLOCK, WIDE), lambda i, s: (jnp.maximum(s[2 * spot + w], 0), 0, i))


def whole(array):
    return pl.BlockSpec(array.shape, lambda i, s: (0,) * array.ndim)


def hard_scores(asked, tables, blocks, spots, mult):
    width = blocks[0].shape[1]
    count, steps = len(spots), width // WIDE

    def body(asked_ref, *refs):
        out, stats = refs[-2:]
        step = pl.program_id(0)

        @pl.when(step == 0)
        def _():
            out[...] = jnp.zeros_like(out)

        for n in range(count):
            query = refs[3 * n][...]
            for w in range(2):
                out[n, w] = out[n, w] + rows_dot(refs[3 * n + 1 + w][0], query)

        @pl.when(step == steps - 1)
        def _():
            for n, spot in enumerate(spots):
                scores = []
                for w in range(2):
                    score = jnp.where(asked_ref[2 * spot + w] >= 0, out[n, w] * mult, LOW)
                    out[n, w] = score
                    scores.append(score)
                peak = jnp.max(jnp.maximum(*scores), axis=0, keepdims=True)
                some = [jnp.where(score > 0.5 * LOW, jnp.exp(score - peak), 0.0) for score in scores]
                stats[n, 0:1] = peak
                stats[n, 1:2] = jnp.sum(some[0] + some[1], axis=0, keepdims=True)

    arrays, specs = [], []
    for block, spot in zip(blocks, spots):
        arrays += [block, *tables]
        specs += [column(block, WIDE), chosen(spot, 0), chosen(spot, 1)]
    outs = [jax.ShapeDtypeStruct((count, 2, BLOCK, BLOCK), F32), jax.ShapeDtypeStruct((count, 2, BLOCK), F32)]
    return kernel(body, asked, arrays, specs, outs, [whole(o) for o in outs], steps)


def hard_parts(asked, scores, norm, tables, plan, peers=None, loop=()):
    width = tables[0].shape[2]
    count = len(plan)
    extra = [a for _, adds, _ in plan for a, _ in adds]
    tail = (() if peers is None else (peers,)) + tuple(loop)

    def body(asked_ref, norm_ref, *refs):
        mine, outs, held = refs[: 3 * count], refs[-count - 1 : -1], refs[-1]
        more = list(refs[3 * count : 3 * count + len(extra)])
        rest = list(refs[3 * count + len(extra) : -count - 1])
        peers_ref = None if peers is None else rest.pop(0)

        @pl.when(pl.program_id(0) == 0)
        def _():
            for n, (spot, _, _) in enumerate(plan):
                for w in range(2):
                    score = mine[3 * n][0, w]
                    weight = jnp.where(score > 0.5 * LOW, jnp.exp(score - norm_ref[spot : spot + 1, :]), 0.0)
                    held[n, :, w * BLOCK : (w + 1) * BLOCK] = weight.T.astype(BF16)

        for n, (spot, adds, dtype) in enumerate(plan):
            keys = jnp.concatenate([mine[3 * n + 1][0], mine[3 * n + 2][0]], axis=0)
            total = mm(held[n], keys)
            for _, peer in adds:
                piece = more.pop(0)[...].astype(F32)
                if peer is not None:
                    scale = jnp.exp(peers_ref[peer : peer + 1, :] - norm_ref[spot : spot + 1, :])
                    piece = piece * jnp.broadcast_to(scale, (BLOCK, BLOCK)).T[:, :1]
                total = total + piece
            if n == 0 and loop:
                for m in range(len(loop) - 1):
                    total = total + mm(rest[0][:, m * BLOCK : (m + 1) * BLOCK], rest[m + 1][...])
            outs[n][...] = total.astype(dtype)

    arrays, specs = [], []
    for spot, _, _ in plan:
        array, n = scores[spot]
        arrays += [array, *tables]
        specs += [
            pl.BlockSpec((1, 2, BLOCK, BLOCK), lambda i, s, n=n: (n, 0, 0, 0)), chosen(spot, 0), chosen(spot, 1),
        ]
    arrays += extra + list(tail)
    specs += [column(a, WIDE) for a in extra] + [whole(a) for a in tail[: len(tail) - max(len(loop) - 1, 0)]]
    specs += [column(a, WIDE) for a in loop[1:]]
    outs = [jax.ShapeDtypeStruct((BLOCK, width), dtype) for _, _, dtype in plan]
    return kernel(
        body, asked, (norm, *arrays), [whole(norm)] + specs, outs, [column(o, WIDE) for o in outs], width // WIDE,
        (pltpu.VMEM((count, BLOCK, 2 * BLOCK), BF16),),
    )


def corpus_part(asked, scores, norm, blocks, held, dtype, w, start=None):
    width = blocks[0].shape[1]
    count = len(blocks)
    arrays = []
    for array, _ in scores:
        if not any(array is a for a in arrays):
            arrays.append(array)
    place = [([array is a for a in arrays].index(True), n) for array, n in scores]

    def body(asked_ref, norm_ref, *refs):
        out, total, weights = refs[-3:]
        found, rest = refs[: len(arrays)], refs[len(arrays) :]

        @pl.when(pl.program_id(0) == 0)
        def _():
            for j, (k, n) in enumerate(place):
                score = found[k][n, w]
                weight = jnp.where(score > 0.5 * LOW, jnp.exp(score - norm_ref[j : j + 1, :]), 0.0)
                weights[j] = weight.astype(BF16)

        total[...] = jnp.zeros_like(total) if start is None else rest[count][...].astype(F32)
        for j in range(count):
            h = jnp.maximum(asked_ref[2 * j + w], 0)
            total[h] = total[h] + mm(weights[j], rest[j][...])
        out[...] = (total[...] * (1 if start is None else OUT_SCALE)).astype(dtype)

    more = () if start is None else (start,)
    out = jax.ShapeDtypeStruct((held, BLOCK, width), dtype)
    return kernel(
        body, asked, (norm, *arrays, *blocks, *more),
        [whole(a) for a in (norm, *arrays)] + [column(a, CHUNK) for a in (*blocks, *more)],
        out, column(out, CHUNK), width // CHUNK,
        (pltpu.VMEM((held, BLOCK, CHUNK), F32), pltpu.VMEM((count, BLOCK, BLOCK), BF16)),
    )


def local(queries, positives, corpus, hard_ids):
    rows, width = queries.shape
    held = corpus.shape[0] // BLOCK
    mult = SCALE / math.sqrt(width)
    me = lax.axis_index("dp")
    turn = 1 - 2 * (me % 2)

    owner = hard_ids[0] // held % 16
    matches = owner[:, None] == jnp.arange(16, dtype=jnp.int32)[None, :]
    wanted = jnp.sum(jnp.where(matches, (hard_ids[0] % held)[:, None] + 1, 0), axis=0) - 1
    pair = wanted[None]
    pair = cat(pair, send(pair, X_LO))
    ring = (pair, send(pair, Y_BWD), send(pair, Y_TWO), send(pair, Y_FWD))
    known = jnp.stack(ring, axis=1).reshape(8, 16)
    every = jnp.arange(16, dtype=jnp.int32)[None, :]
    asked = jnp.stack(
        [jnp.sum(jnp.where(every == place, known, 0), axis=1) for place in (me, me + turn)], axis=1
    )
    asked = jnp.clip(asked.reshape(16), -1, held - 1)

    q, p = {(0, 0): queries}, {(0, 0): positives}
    other = send(corpus, CORE)
    q[1, 0] = send(queries, X_LO)
    q[0, 3], q[0, 1] = send(queries, Y_FWD), send(queries, Y_BWD)
    p[0, 3] = send(after(positives, asked), Z_FWD)

    p[1, 0] = send(after(positives, q[1, 0], other), X_HI)
    q[1, 3] = send(after(q[1, 0], other), Y_FWD)
    q[1, 1] = send(after(q[1, 0], other), Y_BWD)
    p[0, 2] = send(after(p[0, 3], other), Z_FWD)
    p[0, 1] = send(after(positives, q[0, 1], q[0, 3], other), Z_BWD)

    q[0, 2] = send(after(q[0, 3], q[1, 3]), Y_FWD)
    q[1, 2] = send(q[1, 1], Y_BWD)
    p[1, 3], p[1, 1] = send(p[1, 0], Z_FWD), send(after(p[1, 0], p[0, 1]), Z_BWD)
    p[1, 2] = send(after(p[0, 2], p[1, 0]), X_HI)


    tables = (corpus.reshape(held, BLOCK, width), other.reshape(held, BLOCK, width))
    scores, stats = {}, {}
    for group in ([(0, 0), (1, 0), (0, 3), (0, 1), (1, 3), (1, 1)], [(0, 2), (1, 2)]):
        spots = [SPOTS.index(o) for o in group]
        out, stat = hard_scores(asked, tables, [q[o] for o in group], spots, mult)
        for n, j in enumerate(spots):
            scores[j], stats[j] = (out, n), stat[n]
    inner = cat(*[rows_dot(p[o], queries) for o in SPOTS]) * mult
    peak = jnp.max(inner, axis=0)
    total = jnp.sum(jnp.exp(inner - peak[None]), axis=0)
    row = lax.broadcasted_iota(jnp.int32, inner.shape, 0)
    col = lax.broadcasted_iota(jnp.int32, inner.shape, 1)
    diag = row == col
    own_score = jnp.sum(jnp.where(diag, inner, 0.0), axis=0)

    def merge(one, two):
        m = jnp.maximum(one[:, 0], two[:, 0])
        s = one[:, 1] * jnp.exp(one[:, 0] - m) + two[:, 1] * jnp.exp(two[:, 0] - m)
        return jnp.stack([m, s], axis=1)

    state = jnp.stack([stats[j] for j in range(8)])
    peaks = state[:, 0]
    near_spot, far_spot = SPOTS.index((0, 2)), SPOTS.index((1, 2))
    state = cat(merge(state[:1], jnp.stack([peak, total])[None]), state[1:])

    def turned(peer, turns):
        return jnp.roll(peer.reshape(2, 4, 2, BLOCK), turns, axis=(0, 1)).reshape(8, 2, BLOCK)

    state = merge(state, turned(send(state, X_LO), (1, 0)))
    behind = send(cat(state, stats[near_spot][None]), Y_FWD)
    ahead = send(cat(state, stats[far_spot][None]), Y_BWD)
    across = send(state, Y_TWO)
    peers = cat(behind[8:, 0], ahead[8:, 0])
    state = merge(merge(state, turned(ahead[:8], (0, 1))), merge(turned(behind[:8], (0, 3)), turned(across, (0, 2))))
    norm = state[:, 0] + jnp.log(state[:, 1])
    inner_w = (jnp.exp(inner - norm[:1]) - diag.astype(F32)).astype(BF16)
    losses = norm[0] - own_score

    def y_parts(reference, wait, *plan, **more):
        return hard_parts(
            asked, scores, after(reference, *wait), tables,
            [(SPOTS.index(o), adds, dtype) for o, adds, dtype in plan], **more
        )

    def z_part(o, weights, *adds):
        j = SPOTS.index(o)
        return near(mm(weights[j * BLOCK : (j + 1) * BLOCK], queries), *adds).astype(BF16)

    y02, y12 = y_parts(peaks, (), ((0, 2), (), BF16), ((1, 2), (), BF16))
    y02, y12 = send(after(y02, across), Y_FWD), send(after(y12, across), Y_BWD)
    z12 = send(z_part((1, 2), inner_w), X_HI)
    z11 = send(z_part((1, 1), inner_w), Z_FWD)
    z13 = send(z_part((1, 3), inner_w), Z_BWD)

    q_blocks = [q[o] for o in SPOTS]
    in_order = [scores[j] for j in range(8)]
    theirs = corpus_part(asked, in_order, norm, q_blocks, held, BF16, 1)
    y11, y13 = y_parts(norm, (y02, y12), ((1, 1), (), BF16), ((1, 3), ((y12, 1),), BF16), peers=peers)
    inner_2 = after(inner_w, y11)
    y11, y13 = send(y11, Y_FWD), send(y13, Y_BWD)
    z02 = send(z_part((0, 2), inner_2, z12), Z_FWD)
    z10 = send(z_part((1, 0), inner_2, z11, z13), X_HI)
    theirs = send(after(theirs, inner_2, z12, z11, z13), CORE)

    inner_3 = after(inner_2, z02, theirs)
    z01 = send(z_part((0, 1), inner_3, z02), Z_FWD)
    z03 = send(z_part((0, 3), inner_3), Z_BWD)
    loop = (jnp.swapaxes(inner_3, 0, 1), *[p[o] for o in SPOTS])
    (mine,) = y_parts(norm, (z02, theirs), ((0, 0), (), F32), loop=loop)
    y10, y01, y03 = y_parts(
        norm, (y11, y13, mine), ((1, 0), ((y11, None), (y13, None)), BF16), ((0, 1), ((y02, 0),), BF16),
        ((0, 3), (), BF16), peers=peers
    )
    y10 = send(after(y10, z10), X_LO)
    y01, y03 = send(y01, Y_FWD), send(y03, Y_BWD)
    grad_corpus = corpus_part(asked, in_order, after(norm, z03), q_blocks, held, F32, 0, theirs)
    mine, first, grad_corpus = lax.optimization_barrier((mine, mm(inner_3[:BLOCK], queries), grad_corpus))
    grad_queries = OUT_SCALE * near(mine, y01, y03, y10)
    grad_positives = OUT_SCALE * near(first, z01, z03, z10)
    return grad_queries, grad_positives, grad_corpus.reshape(held * BLOCK, width), losses


def solution(mesh):
    spec = P(AXES, None)
    return jax.shard_map(
        local,
        mesh=mesh,
        in_specs=(spec,) * 4,
        out_specs=(spec, spec, spec, P(AXES)),
        check_vma=False,
    )
```

```python
import math

import jax
import jax.numpy as jnp
from jax import lax
from jax.experimental import pallas as pl
from jax.experimental.pallas import tpu as pltpu
from jax.sharding import PartitionSpec as P

BLOCK = 128
SCALE = 3.0
OUT_SCALE = 0.25
LOW = -1e30
CHUNK = 512
WIDE = 1536
AXES = ("blk", "dp")
F32 = jnp.float32
BF16 = jnp.bfloat16


def routes(move):
    pairs = []
    for i in range(128):
        b, d = i // 16, i % 16
        h, z, l, y, c = move(b // 4, b % 4, d // 8, (d // 2) % 4, d % 2)
        pairs.append((i, ((h % 2) * 4 + z % 4) * 16 + (l % 2) * 8 + (y % 4) * 2 + c % 2))
    return pairs


def way(c):
    return 1 - 2 * c


Y_FWD = routes(lambda h, z, l, y, c: (h, z, l, y + way(c), c))
Y_BWD = routes(lambda h, z, l, y, c: (h, z, l, y - way(c), c))
Z_FWD = routes(lambda h, z, l, y, c: (h, z + way(c), l, y, c))
Z_BWD = routes(lambda h, z, l, y, c: (h, z - way(c), l, y, c))
X_LO = routes(lambda h, z, l, y, c: (h, z, l + 1, y, c))
X_HI = routes(lambda h, z, l, y, c: (h + 1, z, l, y, c))
CORE = routes(lambda h, z, l, y, c: (h, z, l, y, c + 1))
Y_TWO = routes(lambda h, z, l, y, c: (h, z, l, y + 2, c))

SPOTS = [(dx, dr) for dx in range(2) for dr in range(4)]


def send(value, route):
    return lax.ppermute(value, AXES, route)


def after(value, *others):
    return lax.optimization_barrier((value, *others))[0]


def cat(*values):
    return jnp.concatenate(values, axis=0)


def rows_dot(left, right):
    return lax.dot_general(left, right, (((1,), (1,)), ((), ())), preferred_element_type=F32)


def mm(left, right):
    return jnp.dot(left, right, preferred_element_type=F32)


def near(value, *others):
    total = value.astype(F32)
    for other in others:
        total = total + other.astype(F32)
    return total


def column(array, chunk):
    if array.ndim == 2:
        return pl.BlockSpec((array.shape[0], chunk), lambda i, s: (0, i))
    return pl.BlockSpec((array.shape[0], array.shape[1], chunk), lambda i, s: (0, 0, i))


def kernel(body, slots, arrays, specs, out, out_spec, steps, scratch=()):
    return pl.pallas_call(
        body,
        grid_spec=pltpu.PrefetchScalarGridSpec(
            num_scalar_prefetch=1, grid=(steps,), in_specs=specs, out_specs=out_spec, scratch_shapes=scratch
        ),
        out_shape=out,
        compiler_params=pltpu.CompilerParams(vmem_limit_bytes=18 * 1024 * 1024),
        cost_estimate=pl.CostEstimate(flops=1024, bytes_accessed=1024, transcendentals=0),
    )(slots, *arrays)


def chosen(spot, w):
    return pl.BlockSpec((1, BLOCK, WIDE), lambda i, s: (jnp.maximum(s[2 * spot + w], 0), 0, i))


def whole(array):
    return pl.BlockSpec(array.shape, lambda i, s: (0,) * array.ndim)


def hard_scores(asked, tables, blocks, spots, mult):
    width = blocks[0].shape[1]
    count, steps = len(spots), width // WIDE

    def body(asked_ref, *refs):
        out, stats = refs[-2:]
        step = pl.program_id(0)

        @pl.when(step == 0)
        def _():
            out[...] = jnp.zeros_like(out)

        for n in range(count):
            query = refs[3 * n][...]
            for w in range(2):
                out[n, w] = out[n, w] + rows_dot(refs[3 * n + 1 + w][0], query)

        @pl.when(step == steps - 1)
        def _():
            for n, spot in enumerate(spots):
                scores = []
                for w in range(2):
                    score = jnp.where(asked_ref[2 * spot + w] >= 0, out[n, w] * mult, LOW)
                    out[n, w] = score
                    scores.append(score)
                peak = jnp.max(jnp.maximum(*scores), axis=0, keepdims=True)
                some = [jnp.where(score > 0.5 * LOW, jnp.exp(score - peak), 0.0) for score in scores]
                stats[n, 0:1] = peak
                stats[n, 1:2] = jnp.sum(some[0] + some[1], axis=0, keepdims=True)

    arrays, specs = [], []
    for block, spot in zip(blocks, spots):
        arrays += [block, *tables]
        specs += [column(block, WIDE), chosen(spot, 0), chosen(spot, 1)]
    outs = [jax.ShapeDtypeStruct((count, 2, BLOCK, BLOCK), F32), jax.ShapeDtypeStruct((count, 2, BLOCK), F32)]
    return kernel(body, asked, arrays, specs, outs, [whole(o) for o in outs], steps)


def hard_parts(asked, scores, norm, tables, plan, peers=None, loop=()):
    width = tables[0].shape[2]
    count = len(plan)
    extra = [a for _, adds, _ in plan for a, _ in adds]
    tail = (() if peers is None else (peers,)) + tuple(loop)

    def body(asked_ref, norm_ref, *refs):
        mine, outs, held = refs[: 3 * count], refs[-count - 1 : -1], refs[-1]
        more = list(refs[3 * count : 3 * count + len(extra)])
        rest = list(refs[3 * count + len(extra) : -count - 1])
        peers_ref = None if peers is None else rest.pop(0)

        @pl.when(pl.program_id(0) == 0)
        def _():
            for n, (spot, _, _) in enumerate(plan):
                for w in range(2):
                    score = mine[3 * n][0, w]
                    weight = jnp.where(score > 0.5 * LOW, jnp.exp(score - norm_ref[spot : spot + 1, :]), 0.0)
                    held[n, :, w * BLOCK : (w + 1) * BLOCK] = weight.T.astype(BF16)

        for n, (spot, adds, dtype) in enumerate(plan):
            keys = jnp.concatenate([mine[3 * n + 1][0], mine[3 * n + 2][0]], axis=0)
            total = mm(held[n], keys)
            for _, peer in adds:
                piece = more.pop(0)[...].astype(F32)
                if peer is not None:
                    scale = jnp.exp(peers_ref[peer : peer + 1, :] - norm_ref[spot : spot + 1, :])
                    piece = piece * jnp.broadcast_to(scale, (BLOCK, BLOCK)).T[:, :1]
                total = total + piece
            if n == 0 and loop:
                for m in range(len(loop) - 1):
                    total = total + mm(rest[0][:, m * BLOCK : (m + 1) * BLOCK], rest[m + 1][...])
            outs[n][...] = total.astype(dtype)

    arrays, specs = [], []
    for spot, _, _ in plan:
        array, n = scores[spot]
        arrays += [array, *tables]
        specs += [
            pl.BlockSpec((1, 2, BLOCK, BLOCK), lambda i, s, n=n: (n, 0, 0, 0)), chosen(spot, 0), chosen(spot, 1),
        ]
    arrays += extra + list(tail)
    specs += [column(a, WIDE) for a in extra] + [whole(a) for a in tail[: len(tail) - max(len(loop) - 1, 0)]]
    specs += [column(a, WIDE) for a in loop[1:]]
    outs = [jax.ShapeDtypeStruct((BLOCK, width), dtype) for _, _, dtype in plan]
    return kernel(
        body, asked, (norm, *arrays), [whole(norm)] + specs, outs, [column(o, WIDE) for o in outs], width // WIDE,
        (pltpu.VMEM((count, BLOCK, 2 * BLOCK), BF16),),
    )


def corpus_part(asked, scores, norm, blocks, held, dtype, w, start=None):
    width = blocks[0].shape[1]
    count = len(blocks)
    arrays = []
    for array, _ in scores:
        if not any(array is a for a in arrays):
            arrays.append(array)
    place = [([array is a for a in arrays].index(True), n) for array, n in scores]

    def body(asked_ref, norm_ref, *refs):
        out, total, weights = refs[-3:]
        found, rest = refs[: len(arrays)], refs[len(arrays) :]

        @pl.when(pl.program_id(0) == 0)
        def _():
            for j, (k, n) in enumerate(place):
                score = found[k][n, w]
                weight = jnp.where(score > 0.5 * LOW, jnp.exp(score - norm_ref[j : j + 1, :]), 0.0)
                weights[j] = weight.astype(BF16)

        total[...] = jnp.zeros_like(total) if start is None else rest[count][...].astype(F32)
        for j in range(count):
            h = jnp.maximum(asked_ref[2 * j + w], 0)
            total[h] = total[h] + mm(weights[j], rest[j][...])
        out[...] = (total[...] * (1 if start is None else OUT_SCALE)).astype(dtype)

    more = () if start is None else (start,)
    out = jax.ShapeDtypeStruct((held, BLOCK, width), dtype)
    return kernel(
        body, asked, (norm, *arrays, *blocks, *more),
        [whole(a) for a in (norm, *arrays)] + [column(a, CHUNK) for a in (*blocks, *more)],
        out, column(out, CHUNK), width // CHUNK,
        (pltpu.VMEM((held, BLOCK, CHUNK), F32), pltpu.VMEM((count, BLOCK, BLOCK), BF16)),
    )


def local(queries, positives, corpus, hard_ids):
    rows, width = queries.shape
    held = corpus.shape[0] // BLOCK
    mult = SCALE / math.sqrt(width)
    me = lax.axis_index("dp")
    turn = 1 - 2 * (me % 2)

    owner = hard_ids[0] // held % 16
    matches = owner[:, None] == jnp.arange(16, dtype=jnp.int32)[None, :]
    wanted = jnp.sum(jnp.where(matches, (hard_ids[0] % held)[:, None] + 1, 0), axis=0) - 1
    pair = wanted[None]
    pair = cat(pair, send(pair, X_LO))
    ring = (pair, send(pair, Y_BWD), send(pair, Y_TWO), send(pair, Y_FWD))
    known = jnp.stack(ring, axis=1).reshape(8, 16)
    every = jnp.arange(16, dtype=jnp.int32)[None, :]
    asked = jnp.stack(
        [jnp.sum(jnp.where(every == place, known, 0), axis=1) for place in (me, me + turn)], axis=1
    )
    asked = jnp.clip(asked.reshape(16), -1, held - 1)

    q, p = {(0, 0): queries}, {(0, 0): positives}
    other = send(corpus, CORE)
    q[1, 0] = send(queries, X_LO)
    q[0, 3], q[0, 1] = send(queries, Y_FWD), send(queries, Y_BWD)
    p[0, 3] = send(after(positives, asked), Z_FWD)

    p[1, 0] = send(after(positives, q[1, 0], other), X_HI)
    q[1, 3] = send(after(q[1, 0], other), Y_FWD)
    q[1, 1] = send(after(q[1, 0], other), Y_BWD)
    p[0, 2] = send(after(p[0, 3], other), Z_FWD)
    p[0, 1] = send(after(positives, q[0, 1], q[0, 3], other), Z_BWD)

    q[0, 2] = send(after(q[0, 3], q[1, 3]), Y_FWD)
    q[1, 2] = send(q[1, 1], Y_BWD)
    p[1, 3], p[1, 1] = send(p[1, 0], Z_FWD), send(after(p[1, 0], p[0, 1]), Z_BWD)
    p[1, 2] = send(after(p[0, 2], p[1, 0]), X_HI)


    tables = (corpus.reshape(held, BLOCK, width), other.reshape(held, BLOCK, width))
    scores, stats = {}, {}
    for group in ([(0, 0), (1, 0), (0, 3), (0, 1), (1, 3), (1, 1)], [(0, 2), (1, 2)]):
        spots = [SPOTS.index(o) for o in group]
        out, stat = hard_scores(asked, tables, [q[o] for o in group], spots, mult)
        for n, j in enumerate(spots):
            scores[j], stats[j] = (out, n), stat[n]
    inner = cat(*[rows_dot(p[o], queries) for o in SPOTS]) * mult
    peak = jnp.max(inner, axis=0)
    total = jnp.sum(jnp.exp(inner - peak[None]), axis=0)
    row = lax.broadcasted_iota(jnp.int32, inner.shape, 0)
    col = lax.broadcasted_iota(jnp.int32, inner.shape, 1)
    diag = row == col
    own_score = jnp.sum(jnp.where(diag, inner, 0.0), axis=0)

    def merge(one, two):
        m = jnp.maximum(one[:, 0], two[:, 0])
        s = one[:, 1] * jnp.exp(one[:, 0] - m) + two[:, 1] * jnp.exp(two[:, 0] - m)
        return jnp.stack([m, s], axis=1)

    state = jnp.stack([stats[j] for j in range(8)])
    peaks = state[:, 0]
    near_spot, far_spot = SPOTS.index((0, 2)), SPOTS.index((1, 2))
    state = cat(merge(state[:1], jnp.stack([peak, total])[None]), state[1:])

    def turned(peer, turns):
        return jnp.roll(peer.reshape(2, 4, 2, BLOCK), turns, axis=(0, 1)).reshape(8, 2, BLOCK)

    state = merge(state, turned(send(state, X_LO), (1, 0)))
    behind = send(cat(state, stats[near_spot][None]), Y_FWD)
    ahead = send(cat(state, stats[far_spot][None]), Y_BWD)
    across = send(state, Y_TWO)
    peers = cat(behind[8:, 0], ahead[8:, 0])
    state = merge(merge(state, turned(ahead[:8], (0, 1))), merge(turned(behind[:8], (0, 3)), turned(across, (0, 2))))
    norm = state[:, 0] + jnp.log(state[:, 1])
    inner_w = (jnp.exp(inner - norm[:1]) - diag.astype(F32)).astype(BF16)
    losses = norm[0] - own_score

    def y_parts(reference, wait, *plan, **more):
        return hard_parts(
            asked, scores, after(reference, *wait), tables,
            [(SPOTS.index(o), adds, dtype) for o, adds, dtype in plan], **more
        )

    def z_part(o, weights, *adds):
        j = SPOTS.index(o)
        return near(mm(weights[j * BLOCK : (j + 1) * BLOCK], queries), *adds).astype(BF16)

    y02, y12 = y_parts(peaks, (), ((0, 2), (), BF16), ((1, 2), (), BF16))
    y02, y12 = send(after(y02, across), Y_FWD), send(after(y12, across), Y_BWD)
    z12 = send(z_part((1, 2), inner_w), X_HI)
    z11 = send(z_part((1, 1), inner_w), Z_FWD)
    z13 = send(z_part((1, 3), inner_w), Z_BWD)

    q_blocks = [q[o] for o in SPOTS]
    in_order = [scores[j] for j in range(8)]
    theirs = corpus_part(asked, in_order, norm, q_blocks, held, BF16, 1)
    y11, y13 = y_parts(norm, (y02, y12), ((1, 1), (), BF16), ((1, 3), ((y12, 1),), BF16), peers=peers)
    inner_2 = after(inner_w, y11)
    y11, y13 = send(y11, Y_FWD), send(y13, Y_BWD)
    z02 = send(z_part((0, 2), inner_2, z12), Z_FWD)
    z10 = send(z_part((1, 0), inner_2, z11, z13), X_HI)
    theirs = send(after(theirs, inner_2, z12, z11, z13), CORE)

    inner_3 = after(inner_2, z02, theirs)
    z01 = send(z_part((0, 1), inner_3, z02), Z_FWD)
    z03 = send(z_part((0, 3), inner_3), Z_BWD)
    loop = (jnp.swapaxes(inner_2, 0, 1), *[p[o] for o in SPOTS])
    (mine,) = y_parts(norm, (z13,), ((0, 0), (), F32), loop=loop)
    y10, y01, y03 = y_parts(
        norm, (y11, y13, mine), ((1, 0), ((y11, None), (y13, None)), BF16), ((0, 1), ((y02, 0),), BF16),
        ((0, 3), (), BF16), peers=peers
    )
    y10 = send(y10, X_LO)
    y01, y03 = send(y01, Y_FWD), send(after(y03, z10), Y_BWD)
    grad_corpus = corpus_part(asked, in_order, after(norm, z03), q_blocks, held, F32, 0, theirs)
    mine, first, grad_corpus = lax.optimization_barrier((mine, mm(inner_3[:BLOCK], queries), grad_corpus))
    grad_queries = OUT_SCALE * near(mine, y01, y03, y10)
    grad_positives = OUT_SCALE * near(first, z01, z03, z10)
    return grad_queries, grad_positives, grad_corpus.reshape(held * BLOCK, width), losses


def solution(mesh):
    spec = P(AXES, None)
    return jax.shard_map(
        local,
        mesh=mesh,
        in_specs=(spec,) * 4,
        out_specs=(spec, spec, spec, P(AXES)),
        check_vma=False,
    )
```

```python
import math

import jax
import jax.numpy as jnp
from jax import lax
from jax.experimental import pallas as pl
from jax.experimental.pallas import tpu as pltpu
from jax.sharding import PartitionSpec as P

BLOCK = 128
SCALE = 3.0
OUT_SCALE = 0.25
LOW = -1e30
CHUNK = 1024
WIDE = 1536
AXES = ("blk", "dp")
F32 = jnp.float32
BF16 = jnp.bfloat16


def routes(move):
    pairs = []
    for i in range(128):
        b, d = i // 16, i % 16
        h, z, l, y, c = move(b // 4, b % 4, d // 8, (d // 2) % 4, d % 2)
        pairs.append((i, ((h % 2) * 4 + z % 4) * 16 + (l % 2) * 8 + (y % 4) * 2 + c % 2))
    return pairs


def way(c):
    return 1 - 2 * c


Y_FWD = routes(lambda h, z, l, y, c: (h, z, l, y + way(c), c))
Y_BWD = routes(lambda h, z, l, y, c: (h, z, l, y - way(c), c))
Z_FWD = routes(lambda h, z, l, y, c: (h, z + way(c), l, y, c))
Z_BWD = routes(lambda h, z, l, y, c: (h, z - way(c), l, y, c))
X_LO = routes(lambda h, z, l, y, c: (h, z, l + 1, y, c))
X_HI = routes(lambda h, z, l, y, c: (h + 1, z, l, y, c))
CORE = routes(lambda h, z, l, y, c: (h, z, l, y, c + 1))
Y_TWO = routes(lambda h, z, l, y, c: (h, z, l, y + 2, c))

SPOTS = [(dx, dr) for dx in range(2) for dr in range(4)]


def send(value, route):
    return lax.ppermute(value, AXES, route)


def after(value, *others):
    return lax.optimization_barrier((value, *others))[0]


def cat(*values):
    return jnp.concatenate(values, axis=0)


def rows_dot(left, right):
    return lax.dot_general(left, right, (((1,), (1,)), ((), ())), preferred_element_type=F32)


def mm(left, right):
    return jnp.dot(left, right, preferred_element_type=F32)


def near(value, *others):
    total = value.astype(F32)
    for other in others:
        total = total + other.astype(F32)
    return total


def column(array, chunk):
    if array.ndim == 2:
        return pl.BlockSpec((array.shape[0], chunk), lambda i, s: (0, i))
    return pl.BlockSpec((array.shape[0], array.shape[1], chunk), lambda i, s: (0, 0, i))


def kernel(body, slots, arrays, specs, out, out_spec, steps, scratch=()):
    return pl.pallas_call(
        body,
        grid_spec=pltpu.PrefetchScalarGridSpec(
            num_scalar_prefetch=1, grid=(steps,), in_specs=specs, out_specs=out_spec, scratch_shapes=scratch
        ),
        out_shape=out,
        compiler_params=pltpu.CompilerParams(vmem_limit_bytes=18 * 1024 * 1024),
        cost_estimate=pl.CostEstimate(flops=1024, bytes_accessed=1024, transcendentals=0),
    )(slots, *arrays)


def chosen(spot, w):
    return pl.BlockSpec((1, BLOCK, WIDE), lambda i, s: (jnp.maximum(s[2 * spot + w], 0), 0, i))


def whole(array):
    return pl.BlockSpec(array.shape, lambda i, s: (0,) * array.ndim)


def hard_scores(asked, tables, blocks, spots, mult):
    width = blocks[0].shape[1]
    count, steps = len(spots), width // WIDE

    def body(asked_ref, *refs):
        out, stats = refs[-2:]
        step = pl.program_id(0)

        @pl.when(step == 0)
        def _():
            out[...] = jnp.zeros_like(out)

        for n in range(count):
            query = refs[3 * n][...]
            for w in range(2):
                out[n, w] = out[n, w] + rows_dot(refs[3 * n + 1 + w][0], query)

        @pl.when(step == steps - 1)
        def _():
            for n, spot in enumerate(spots):
                scores = []
                for w in range(2):
                    score = jnp.where(asked_ref[2 * spot + w] >= 0, out[n, w] * mult, LOW)
                    out[n, w] = score
                    scores.append(score)
                peak = jnp.max(jnp.maximum(*scores), axis=0, keepdims=True)
                some = [jnp.where(score > 0.5 * LOW, jnp.exp(score - peak), 0.0) for score in scores]
                stats[n, 0:1] = peak
                stats[n, 1:2] = jnp.sum(some[0] + some[1], axis=0, keepdims=True)

    arrays, specs = [], []
    for block, spot in zip(blocks, spots):
        arrays += [block, *tables]
        specs += [column(block, WIDE), chosen(spot, 0), chosen(spot, 1)]
    outs = [jax.ShapeDtypeStruct((count, 2, BLOCK, BLOCK), F32), jax.ShapeDtypeStruct((count, 2, BLOCK), F32)]
    return kernel(body, asked, arrays, specs, outs, [whole(o) for o in outs], steps)


def hard_parts(asked, scores, norm, tables, plan, peers=None, loop=()):
    width = tables[0].shape[2]
    count = len(plan)
    extra = [a for _, adds, _ in plan for a, _ in adds]
    tail = (() if peers is None else (peers,)) + tuple(loop)

    def body(asked_ref, norm_ref, *refs):
        mine, outs, held = refs[: 3 * count], refs[-count - 1 : -1], refs[-1]
        more = list(refs[3 * count : 3 * count + len(extra)])
        rest = list(refs[3 * count + len(extra) : -count - 1])
        peers_ref = None if peers is None else rest.pop(0)

        @pl.when(pl.program_id(0) == 0)
        def _():
            for n, (spot, _, _) in enumerate(plan):
                for w in range(2):
                    score = mine[3 * n][0, w]
                    weight = jnp.where(score > 0.5 * LOW, jnp.exp(score - norm_ref[spot : spot + 1, :]), 0.0)
                    held[n, :, w * BLOCK : (w + 1) * BLOCK] = weight.T.astype(BF16)

        for n, (spot, adds, dtype) in enumerate(plan):
            keys = jnp.concatenate([mine[3 * n + 1][0], mine[3 * n + 2][0]], axis=0)
            total = mm(held[n], keys)
            for _, peer in adds:
                piece = more.pop(0)[...].astype(F32)
                if peer is not None:
                    scale = jnp.exp(peers_ref[peer : peer + 1, :] - norm_ref[spot : spot + 1, :])
                    piece = piece * jnp.broadcast_to(scale, (BLOCK, BLOCK)).T[:, :1]
                total = total + piece
            if n == 0 and loop:
                for m in range(len(loop) - 1):
                    total = total + mm(rest[0][:, m * BLOCK : (m + 1) * BLOCK], rest[m + 1][...])
            outs[n][...] = total.astype(dtype)

    arrays, specs = [], []
    for spot, _, _ in plan:
        array, n = scores[spot]
        arrays += [array, *tables]
        specs += [
            pl.BlockSpec((1, 2, BLOCK, BLOCK), lambda i, s, n=n: (n, 0, 0, 0)), chosen(spot, 0), chosen(spot, 1),
        ]
    arrays += extra + list(tail)
    specs += [column(a, WIDE) for a in extra] + [whole(a) for a in tail[: len(tail) - max(len(loop) - 1, 0)]]
    specs += [column(a, WIDE) for a in loop[1:]]
    outs = [jax.ShapeDtypeStruct((BLOCK, width), dtype) for _, _, dtype in plan]
    return kernel(
        body, asked, (norm, *arrays), [whole(norm)] + specs, outs, [column(o, WIDE) for o in outs], width // WIDE,
        (pltpu.VMEM((count, BLOCK, 2 * BLOCK), BF16),),
    )


def corpus_part(asked, scores, norm, blocks, held, dtype, w, start=None):
    width = blocks[0].shape[1]
    count = len(blocks)
    arrays = []
    for array, _ in scores:
        if not any(array is a for a in arrays):
            arrays.append(array)
    place = [([array is a for a in arrays].index(True), n) for array, n in scores]

    def body(asked_ref, norm_ref, *refs):
        out, total, weights = refs[-3:]
        found, rest = refs[: len(arrays)], refs[len(arrays) :]

        @pl.when(pl.program_id(0) == 0)
        def _():
            for j, (k, n) in enumerate(place):
                score = found[k][n, w]
                weight = jnp.where(score > 0.5 * LOW, jnp.exp(score - norm_ref[j : j + 1, :]), 0.0)
                weights[j] = weight.astype(BF16)

        total[...] = jnp.zeros_like(total) if start is None else rest[count][...].astype(F32)
        for j in range(count):
            h = jnp.maximum(asked_ref[2 * j + w], 0)
            total[h] = total[h] + mm(weights[j], rest[j][...])
        out[...] = (total[...] * (1 if start is None else OUT_SCALE)).astype(dtype)

    more = () if start is None else (start,)
    out = jax.ShapeDtypeStruct((held, BLOCK, width), dtype)
    return kernel(
        body, asked, (norm, *arrays, *blocks, *more),
        [whole(a) for a in (norm, *arrays)] + [column(a, CHUNK) for a in (*blocks, *more)],
        out, column(out, CHUNK), width // CHUNK,
        (pltpu.VMEM((held, BLOCK, CHUNK), F32), pltpu.VMEM((count, BLOCK, BLOCK), BF16)),
    )


def local(queries, positives, corpus, hard_ids):
    rows, width = queries.shape
    held = corpus.shape[0] // BLOCK
    mult = SCALE / math.sqrt(width)
    me = lax.axis_index("dp")
    turn = 1 - 2 * (me % 2)

    owner = hard_ids[0] // held % 16
    matches = owner[:, None] == jnp.arange(16, dtype=jnp.int32)[None, :]
    wanted = jnp.sum(jnp.where(matches, (hard_ids[0] % held)[:, None] + 1, 0), axis=0) - 1
    pair = wanted[None]
    pair = cat(pair, send(pair, X_LO))
    ring = (pair, send(pair, Y_BWD), send(pair, Y_TWO), send(pair, Y_FWD))
    known = jnp.stack(ring, axis=1).reshape(8, 16)
    every = jnp.arange(16, dtype=jnp.int32)[None, :]
    asked = jnp.stack(
        [jnp.sum(jnp.where(every == place, known, 0), axis=1) for place in (me, me + turn)], axis=1
    )
    asked = jnp.clip(asked.reshape(16), -1, held - 1)

    q, p = {(0, 0): queries}, {(0, 0): positives}
    other = send(corpus, CORE)
    q[1, 0] = send(queries, X_LO)
    q[0, 3], q[0, 1] = send(queries, Y_FWD), send(queries, Y_BWD)
    p[0, 3] = send(after(positives, asked), Z_FWD)

    p[1, 0] = send(after(positives, q[1, 0], other), X_HI)
    q[1, 3] = send(after(q[1, 0], other), Y_FWD)
    q[1, 1] = send(after(q[1, 0], other), Y_BWD)
    p[0, 2] = send(after(p[0, 3], other), Z_FWD)
    p[0, 1] = send(after(positives, q[0, 1], q[0, 3], other), Z_BWD)

    q[0, 2] = send(after(q[0, 3], q[1, 3]), Y_FWD)
    q[1, 2] = send(q[1, 1], Y_BWD)
    p[1, 3], p[1, 1] = send(p[1, 0], Z_FWD), send(after(p[1, 0], p[0, 1]), Z_BWD)
    p[1, 2] = send(after(p[0, 2], p[1, 0]), X_HI)


    tables = (corpus.reshape(held, BLOCK, width), other.reshape(held, BLOCK, width))
    scores, stats = {}, {}
    for group in ([(0, 0), (1, 0), (0, 3), (0, 1), (1, 3), (1, 1)], [(0, 2), (1, 2)]):
        spots = [SPOTS.index(o) for o in group]
        out, stat = hard_scores(asked, tables, [q[o] for o in group], spots, mult)
        for n, j in enumerate(spots):
            scores[j], stats[j] = (out, n), stat[n]
    inner = cat(*[rows_dot(p[o], queries) for o in SPOTS]) * mult
    peak = jnp.max(inner, axis=0)
    total = jnp.sum(jnp.exp(inner - peak[None]), axis=0)
    row = lax.broadcasted_iota(jnp.int32, inner.shape, 0)
    col = lax.broadcasted_iota(jnp.int32, inner.shape, 1)
    diag = row == col
    own_score = jnp.sum(jnp.where(diag, inner, 0.0), axis=0)

    def merge(one, two):
        m = jnp.maximum(one[:, 0], two[:, 0])
        s = one[:, 1] * jnp.exp(one[:, 0] - m) + two[:, 1] * jnp.exp(two[:, 0] - m)
        return jnp.stack([m, s], axis=1)

    state = jnp.stack([stats[j] for j in range(8)])
    peaks = state[:, 0]
    near_spot, far_spot = SPOTS.index((0, 2)), SPOTS.index((1, 2))
    state = cat(merge(state[:1], jnp.stack([peak, total])[None]), state[1:])

    def turned(peer, turns):
        return jnp.roll(peer.reshape(2, 4, 2, BLOCK), turns, axis=(0, 1)).reshape(8, 2, BLOCK)

    state = merge(state, turned(send(state, X_LO), (1, 0)))
    behind = send(cat(state, stats[near_spot][None]), Y_FWD)
    ahead = send(cat(state, stats[far_spot][None]), Y_BWD)
    across = send(state, Y_TWO)
    peers = cat(behind[8:, 0], ahead[8:, 0])
    state = merge(merge(state, turned(ahead[:8], (0, 1))), merge(turned(behind[:8], (0, 3)), turned(across, (0, 2))))
    norm = state[:, 0] + jnp.log(state[:, 1])
    inner_w = (jnp.exp(inner - norm[:1]) - diag.astype(F32)).astype(BF16)
    losses = norm[0] - own_score

    def y_parts(reference, wait, *plan, **more):
        return hard_parts(
            asked, scores, after(reference, *wait), tables,
            [(SPOTS.index(o), adds, dtype) for o, adds, dtype in plan], **more
        )

    def z_part(o, weights, *adds):
        j = SPOTS.index(o)
        return near(mm(weights[j * BLOCK : (j + 1) * BLOCK], queries), *adds).astype(BF16)

    y02, y12 = y_parts(peaks, (), ((0, 2), (), BF16), ((1, 2), (), BF16))
    y02, y12 = send(after(y02, across), Y_FWD), send(after(y12, across), Y_BWD)
    z12 = send(z_part((1, 2), inner_w), X_HI)
    z11 = send(z_part((1, 1), inner_w), Z_FWD)
    z13 = send(z_part((1, 3), inner_w), Z_BWD)

    q_blocks = [q[o] for o in SPOTS]
    in_order = [scores[j] for j in range(8)]
    theirs = corpus_part(asked, in_order, norm, q_blocks, held, BF16, 1)
    y11, y13 = y_parts(norm, (y02, y12), ((1, 1), (), BF16), ((1, 3), ((y12, 1),), BF16), peers=peers)
    inner_2 = after(inner_w, y11)
    y11, y13 = send(y11, Y_FWD), send(y13, Y_BWD)
    z02 = send(z_part((0, 2), inner_2, z12), Z_FWD)
    z10 = send(z_part((1, 0), inner_2, z11, z13), X_HI)
    theirs = send(after(theirs, inner_2, z12, z11, z13), CORE)

    inner_3 = after(inner_2, z02, theirs)
    z01 = send(z_part((0, 1), inner_3, z02), Z_FWD)
    z03 = send(z_part((0, 3), inner_3), Z_BWD)
    loop = (jnp.swapaxes(inner_2, 0, 1), *[p[o] for o in SPOTS])
    (mine,) = y_parts(norm, (z13,), ((0, 0), (), F32), loop=loop)
    y10, y01, y03 = y_parts(
        norm, (y11, y13, mine), ((1, 0), ((y11, None), (y13, None)), BF16), ((0, 1), ((y02, 0),), BF16),
        ((0, 3), (), BF16), peers=peers
    )
    y10 = send(y10, X_LO)
    y01, y03 = send(y01, Y_FWD), send(after(y03, z10), Y_BWD)
    grad_corpus = corpus_part(asked, in_order, after(norm, z03), q_blocks, held, F32, 0, theirs)
    mine, first, grad_corpus = lax.optimization_barrier((mine, mm(inner_3[:BLOCK], queries), grad_corpus))
    grad_queries = OUT_SCALE * near(mine, y01, y03, y10)
    grad_positives = OUT_SCALE * near(first, z01, z03, z10)
    return grad_queries, grad_positives, grad_corpus.reshape(held * BLOCK, width), losses


def solution(mesh):
    spec = P(AXES, None)
    return jax.shard_map(
        local,
        mesh=mesh,
        in_specs=(spec,) * 4,
        out_specs=(spec, spec, spec, P(AXES)),
        check_vma=False,
    )
```
